256 devices in a mesh: stream: 32 (over z, y_lo, core), slab: 8 (over y_hi, x).
Axes of the slice: x: 4, y: 4 (y_hi: 2, y_lo: 2; y = y_hi * 2 + y_lo), z: 8, core: 2. Of those that a mesh axis runs over, the one named last changes fastest.
Arguments:
- conc: float32 [2, 64, 64, 4096], P(None, 'slab', None, 'stream'), may hold values from -6 to 6
- kappa: float32 [2, 64, 64, 4096], P(None, 'slab', None, 'stream'), may hold values from 0.01 to 0.1
- velocity: float32 [64, 64, 4096], P('slab', None, 'stream'), may hold values from 0.02 to 0.2
- cell_type: int32 [64, 64, 4096], P('slab', None, 'stream'), may hold values 0 or 1
- target_row: int32 [2, 64, 4096], P(None, None, 'stream'), may hold values from 0 to 63, as said below
- target_col: int32 [2, 64, 4096], P(None, None, 'stream'), may hold values from 0 to 4095, as said below
- mortar_weight: float32 [2, 64, 4096], P(None, None, 'stream'), may hold values from 0.3 to 1
Outputs:
- final: float32 [2, 64, 64, 4096], P(None, 'slab', None, 'stream')
The draws below stay inside these ranges and needn't reach their ends.
Inputs may be any that keep to these rules, and one draw needn't show every extreme that they name: target_row lies within one cell of the face's lateral index. target_col lies within one cell of the face's streamwise index.
All inputs are finite; a program needn't handle non-finite values. No bound on the sum of `cell_type` on one device may be relied on, other than what follows from the above.
Results may differ from the reference program's by a relative error of at most 0.0001.
Values sent between devices are 32-bit elements; how exact they have to be, the bound alone decides.
No kernel may reach another device: no remote copies, remote signals or barrier semaphores. Data moves between devices by JAX's collectives and lax.ppermute only.
A program may use at most 128 MiB of HBM per device.

```python
import math
import jax
import jax.numpy as jnp

CZ = 8
STEPS = 3
NX = 4096
NY = 64
NZ = 64
N_SLAB = 8


def draw_target_row(key, part):
    key = jax.random.fold_in(key, 11)
    offset = jax.random.randint(key, (2, NY, NX), -1, 2)
    base = jnp.arange(NY, dtype=jnp.int32)[None, :, None]
    return jnp.clip(base + offset, 0, NY - 1).astype(jnp.int32)


def draw_target_col(key, part):
    key = jax.random.fold_in(key, 23)
    offset = jax.random.randint(key, (2, NY, NX), -1, 2)
    base = jnp.arange(NX, dtype=jnp.int32)[None, None, :]
    return jnp.clip(base + offset, 0, NX - 1).astype(jnp.int32)


def set_ends(entries, key, least, top_value):
    dims = entries.shape
    place = [jax.random.randint(jax.random.fold_in(key, axis), (), 0, dims[axis]) for axis in range(len(dims))]
    entries = entries.at[tuple(place)].set(least)
    longest = dims.index(max(dims))
    place[longest] = (place[longest] + 1) % dims[longest]
    return entries.at[tuple(place)].set(top_value)


def levels(key, shape, shards, least, high):
    level = 1.0
    for dim, shards_of in shards:
        heights = jax.random.uniform(jax.random.fold_in(jax.random.fold_in(key, 6), dim), (shards_of,), jnp.float32, least / len(shards), high / len(shards))
        level = level * jnp.repeat(jnp.exp(heights), shape[dim] // shards_of).reshape((-1,) + (1,) * (len(shape) - 1 - dim))
    return level


def gaussian(key, extent, deviation, most, split=(), kind=jnp.bfloat16):
    factor_of = levels(key, extent, split, -0.22, 0.18) if split else 1.0
    entries = jax.random.normal(key, extent, jnp.float32) * deviation * factor_of
    return jnp.minimum(jnp.maximum(entries, -most), most).astype(kind)


def setup_inputs(seed: int = 0) -> dict:
    keys = jax.random.split(jax.random.key(seed), 8)
    conc = gaussian(keys[0], (2, NZ, NY, NX), 1.0, 6.0, ((1, 8), (3, 32)), jnp.float32)
    kappa = jnp.clip(jnp.exp(math.log(0.1) - 2.3025851 * jax.random.uniform(keys[1], (2, NZ, NY, NX), jnp.float32) ** levels(keys[1], (2, NZ, NY, NX), ((1, 8), (3, 32)), -0.2, 0.2)), 0.01, 0.1)
    velocity = jnp.clip(0.02 + 0.18 * jax.random.uniform(keys[2], (NZ, NY, NX), jnp.float32) ** levels(keys[2], (NZ, NY, NX), ((0, 8), (2, 32)), -0.2, 0.2), 0.02, 0.2)
    cell_type = set_ends((jax.random.randint(keys[3], (NZ, NY, NX), 0, 10) < 9).astype(jnp.int32), jax.random.fold_in(keys[3], 1), 0, 1)
    target_row = draw_target_row(jax.random.fold_in(keys[7], 71), 0)
    target_col = draw_target_col(jax.random.fold_in(keys[7], 71), 0)
    mortar_weight = jnp.clip(0.3 + 0.7 * jax.random.uniform(keys[6], (2, NY, NX), jnp.float32) ** levels(keys[6], (2, NY, NX), ((2, 32),), -0.2, 0.2), 0.3, 1.0)
    return {"conc": conc, "kappa": kappa, "velocity": velocity, "cell_type": cell_type, "target_row": target_row, "target_col": target_col, "mortar_weight": mortar_weight}


def transport(pc, pk, pu):
    cx = pc[:, 1:-1]
    kx = pk[:, 1:-1]
    fx = 0.5 * (kx[..., 1:] + kx[..., :-1]) * (cx[..., 1:] - cx[..., :-1])
    diff_x = fx[..., 1:] - fx[..., :-1]
    cz = pc[..., 1:-1]
    kz = pk[..., 1:-1]
    fz = 0.5 * (kz[:, 1:] + kz[:, :-1]) * (cz[:, 1:] - cz[:, :-1])
    diff_z = fz[:, 1:] - fz[:, :-1]
    cell = pc[:, 1:-1, :, 1:-1]
    kcell = pk[:, 1:-1, :, 1:-1]
    fy = 0.5 * (kcell[:, :, 1:] + kcell[:, :, :-1]) * (cell[:, :, 1:] - cell[:, :, :-1])
    zero_row = jnp.zeros_like(fy[:, :, :1])
    diff_y = jnp.concatenate([fy, zero_row], 2) - jnp.concatenate([zero_row, fy], 2)
    carried = pu[None, 1:-1] * pc[:, 1:-1]
    advect = carried[..., :-2] - carried[..., 1:-1]
    return diff_x + diff_y + diff_z + advect


def face_flux(water, bed_wide, offsets, weights, rates):
    rows = water.shape[-2]
    count = water.shape[-1]
    lead = [(0, 0)] * (water.ndim - 2)
    padded = jnp.pad(bed_wide, lead + [(1, 1), (0, 0)])
    totals = [jnp.zeros_like(water), jnp.zeros_like(water)]
    for shift_a in (-1, 0, 1):
        for shift_b in (-1, 0, 1):
            moved = padded[..., 1 + shift_a:1 + shift_a + rows, 1 + shift_b:1 + shift_b + count]
            for intersection in range(2):
                hit = ((offsets[intersection] == shift_a) & (offsets[2 + intersection] == shift_b)).astype(water.dtype)
                totals[intersection] = totals[intersection] + hit * moved
    scale = rates.reshape((rates.shape[0],) + (1,) * (water.ndim - 1))
    parts = [scale * weights[intersection] * (water - totals[intersection]) for intersection in range(2)]
    return jnp.stack(parts, 1)


def spread(flux, offsets):
    rows = flux.shape[-2]
    count = flux.shape[-1]
    lead = [(0, 0)] * (flux.ndim - 3)
    wide = jnp.zeros(flux.shape[:1] + flux.shape[2:-1] + (count + 2,), flux.dtype)
    for shift_a in (-1, 0, 1):
        for shift_b in (-1, 0, 1):
            part = jnp.zeros_like(flux[:, 0])
            for intersection in range(2):
                hit = ((offsets[intersection] == shift_a) & (offsets[2 + intersection] == shift_b)).astype(flux.dtype)
                part = part + hit * flux[:, intersection]
            moved = jnp.pad(part, lead + [(1, 1), (0, 0)])[..., 1 - shift_a:1 - shift_a + rows, :]
            wide = wide + jnp.pad(moved, lead + [(0, 0), (1 + shift_b, 1 - shift_b)])
    return wide


def reference(conc, kappa, velocity, cell_type, target_row, target_col, mortar_weight):
    rates = jnp.array([0.08, 0.12], conc.dtype)
    active = cell_type.astype(conc.dtype)
    row_off = (target_row - jnp.arange(NY, dtype=jnp.int32)[None, :, None]).astype(conc.dtype)
    col_off = (target_col - jnp.arange(NX, dtype=jnp.int32)[None, None, :]).astype(conc.dtype)
    offsets = jnp.concatenate([row_off, col_off], 0)
    pk = jnp.pad(kappa, ((0, 0), (1, 1), (0, 0), (1, 1)))
    pu = jnp.pad(velocity, ((1, 1), (0, 0), (1, 1)))
    for step in range(STEPS):
        pc = jnp.pad(conc, ((0, 0), (1, 1), (0, 0), (1, 1)))
        delta = transport(pc, pk, pu)
        for bound in range(1, N_SLAB):
            upper = bound * CZ - 1
            water = conc[:, upper]
            bed_wide = jnp.pad(conc[:, upper + 1], ((0, 0), (0, 0), (1, 1)))
            flux = face_flux(water, bed_wide, offsets, mortar_weight, rates)
            loss = jnp.sum(flux, axis=1)
            gain = spread(flux, offsets)[..., 1:-1]
            delta = delta.at[:, upper].add(-loss).at[:, upper + 1].add(gain)
        conc = conc + active[None] * delta
    return conc
```

```python
import jax
import jax.numpy as jnp
from jax import lax
from jax.experimental import pallas as pl
from jax.experimental.pallas import tpu as pltpu
from jax.sharding import PartitionSpec as P

RATES = (0.08, 0.12)
DEPTH, ROWS, COLS = 8, 64, 128
WIDE = 2 * COLS
HALO = 3
GROUP = 2 * HALO
SLOTS = COLS // GROUP
PLANES = 12
G_CONC, G_KAPPA, G_VEL, G_TYPE, G_FACE, GROUPS = 0, 16, 32, 40, 48, 54
TILES = -(-GROUPS // SLOTS)


def lanes_of(shape):
    return lax.broadcasted_iota(jnp.int32, shape, len(shape) - 1)


def edge_mask():
    lane = lanes_of((ROWS, COLS))
    return (lane < HALO) | (lane >= COLS - HALO)


def place_group(tile, plane, slot):
    lane = lanes_of(tile.shape)
    start = slot * GROUP
    moved = pltpu.roll(plane, (start + HALO) % COLS, 1)
    return jnp.where((lane >= start) & (lane < start + GROUP), moved, tile)


def take_group(tile, slot):
    moved = pltpu.roll(tile, (COLS - slot * GROUP - HALO) % COLS, 1)
    return jnp.where(edge_mask(), moved, 0.0)


def wide(main, halo):
    return jnp.concatenate([main, halo], axis=1)


def shift_cols(x, by):
    return pltpu.roll(x, (-by) % x.shape[1], 1)


def shift_rows(x, by):
    return pltpu.roll(x, (-by) % x.shape[0], 0)


def in_plane(c, kx, ky, v):
    s = kx * (shift_cols(c, 1) - c) - v * c
    f = ky * (shift_rows(c, 1) - c)
    return (s - shift_cols(s, -1)) + (f - shift_rows(f, -1))


def face_x(k):
    return 0.5 * (k + shift_cols(k, 1))


def face_y(k):
    row = lax.broadcasted_iota(jnp.int32, k.shape, 0)
    return jnp.where(row < ROWS - 1, 0.5 * (k + shift_rows(k, 1)), 0.0)


def gather(m_ref, bed):
    total = None
    for b in (-1, 0, 1):
        at_b = shift_cols(bed, b) if b else bed
        for a in (-1, 0, 1):
            term = m_ref[3 * (a + 1) + b + 1] * (shift_rows(at_b, a) if a else at_b)
            total = term if total is None else total + term
    return total


def scatter(m_ref, water):
    total = None
    for b in (-1, 0, 1):
        part = None
        for a in (-1, 0, 1):
            term = m_ref[3 * (a + 1) + b + 1]
            if water is not None:
                term = term * water
            term = shift_rows(term, -a) if a else term
            part = term if part is None else part + term
        part = shift_cols(part, -b) if b else part
        total = part if total is None else total + part
    return total


def face_planes(row_ref, col_ref, w_ref):
    start = lax.axis_index("stream") * COLS
    row = lax.broadcasted_iota(jnp.int32, (ROWS, COLS), 0)
    col = lanes_of((ROWS, COLS)) + start
    out = [(row_ref[k] - row).astype(jnp.float32) for k in range(2)]
    out += [(col_ref[k] - col).astype(jnp.float32) for k in range(2)]
    return out + [w_ref[k] for k in range(2)]


def pack_kernel(conc, kappa, vel, kind, row_ref, col_ref, w_ref, msg):
    tiles = [jnp.zeros((ROWS, COLS), jnp.float32) for _ in range(TILES)]

    def put(group, plane):
        t, slot = divmod(group, SLOTS)
        tiles[t] = place_group(tiles[t], plane, slot)

    for q in range(2):
        for z in range(DEPTH):
            put(G_CONC + q * DEPTH + z, conc[q, z])
            put(G_KAPPA + q * DEPTH + z, kappa[q, z])
    for z in range(DEPTH):
        put(G_VEL + z, vel[z])
        put(G_TYPE + z, kind[z].astype(jnp.float32))
    for i, plane in enumerate(face_planes(row_ref, col_ref, w_ref)):
        put(G_FACE + i, plane)
    for t in range(TILES):
        msg[t] = tiles[t]


def block_kernel(
    conc, kappa, vel, kind, row_ref, col_ref, w_ref, got_a, got_b,
    u3, msg_a, msg_b, halo, edge_u, m_out,
    cells, kx, ky, kz, own,
):
    even = lax.axis_index("stream") % 2 == 0
    lane = lanes_of((ROWS, COLS))
    low = lax.rem(lane, GROUP) < HALO
    from_b = low == even
    for t in range(TILES):
        both = jnp.where(from_b, got_b[t], got_a[t])
        for slot in range(min(SLOTS, GROUPS - t * SLOTS)):
            halo[t * SLOTS + slot] = take_group(both, slot)

    planes = [wide(p, halo[G_FACE + i]) for i, p in enumerate(face_planes(row_ref, col_ref, w_ref))]
    for a in (-1, 0, 1):
        for b in (-1, 0, 1):
            total = None
            for k in range(2):
                term = jnp.where((planes[k] == a) & (planes[2 + k] == b), planes[4 + k], 0.0)
                total = term if total is None else total + term
            m_out[3 * (a + 1) + b + 1] = total
    slab = lax.axis_index("slab")
    upper = (slab > 0).astype(jnp.float32)
    lower = (slab < lax.axis_size("slab") - 1).astype(jnp.float32)
    m_out[9] = scatter(m_out, None)
    m_out[10] = planes[4] + planes[5]

    own[...] = jnp.zeros(own.shape, jnp.float32)
    own[0] = m_out[9] * upper
    own[DEPTH - 1] = m_out[10] * lower

    def prepare(z, _):
        for q in range(2):
            k = wide(kappa[q, z], halo[G_KAPPA + q * DEPTH + z])
            kx[q, z] = face_x(k)
            ky[q, z] = face_y(k)
            cells[0, q, z + 1] = wide(conc[q, z], halo[G_CONC + q * DEPTH + z])
        return 0

    lax.fori_loop(0, DEPTH, prepare, 0)

    def prepare_z(z, _):
        for q in range(2):
            k = wide(kappa[q, z], halo[G_KAPPA + q * DEPTH + z])
            below = wide(kappa[q, z + 1], halo[G_KAPPA + q * DEPTH + z + 1])
            kz[q, z + 1] = 0.5 * (k + below)
        return 0

    lax.fori_loop(0, DEPTH - 1, prepare_z, 0)
    zeros = jnp.zeros((ROWS, WIDE), jnp.float32)
    for q in range(2):
        kz[q, 0] = zeros
        kz[q, DEPTH] = zeros
        for t in range(2):
            cells[t, q, 0] = zeros
            cells[t, q, DEPTH + 1] = zeros

    for step in range(3):
        now, later = step % 2, (step + 1) % 2

        def advance(z, _):
            a = wide(kind[z].astype(jnp.float32), halo[G_TYPE + z])
            v = wide(vel[z], halo[G_VEL + z])
            for q in range(2):
                c = cells[now, q, z + 1]
                r = in_plane(c, kx[q, z], ky[q, z], v)
                r += kz[q, z + 1] * (cells[now, q, z + 2] - c)
                r -= kz[q, z] * (c - cells[now, q, z])
                r -= RATES[q] * own[z] * c
                new = c + a * r
                if step == 2:
                    u3[q, z] = new[:, :COLS]
                else:
                    cells[later, q, z + 1] = new
            return 0

        lax.fori_loop(0, DEPTH, advance, 0)
        if step < 2:
            for q in range(2):
                edge_u[0, step, q] = cells[later, q, 1]
                edge_u[1, step, q] = cells[later, q, DEPTH]

    slab_even = slab % 2 == 0

    def sides(layers):
        first, second = layers
        out = []
        for q in range(2):
            out.append((conc[q, first], halo[G_CONC + q * DEPTH + first]))
        side = 0 if first == 0 else 1
        for t in range(2):
            for q in range(2):
                u = edge_u[side, t, q]
                out.append((u[:, :COLS], u[:, COLS:]))
        for z in (first, second):
            for q in range(2):
                out.append((kappa[q, z], halo[G_KAPPA + q * DEPTH + z]))
        out.append((vel[first], halo[G_VEL + first]))
        out.append((kind[first].astype(jnp.float32), halo[G_TYPE + first]))
        return out

    strip_a = jnp.zeros((ROWS, COLS), jnp.float32)
    strip_b = strip_a
    for i, (top, bottom) in enumerate(zip(sides((0, 1)), sides((DEPTH - 1, DEPTH - 2)))):
        msg_a[i] = jnp.where(slab_even, bottom[0], top[0])
        msg_b[i] = jnp.where(slab_even, top[0], bottom[0])
        strip_a = place_group(strip_a, jnp.where(slab_even, bottom[1], top[1]), i)
        strip_b = place_group(strip_b, jnp.where(slab_even, top[1], bottom[1]), i)
    msg_a[PLANES] = strip_a
    msg_b[PLANES] = strip_b


def join_kernel(conc, kappa, vel, kind, halo, edge_u, m_ref, u3, got_a, got_b, out, ghost):
    slab = lax.axis_index("slab")
    slab_even = slab % 2 == 0
    upper = (slab > 0).astype(jnp.float32)
    lower = (slab < lax.axis_size("slab") - 1).astype(jnp.float32)
    for side in range(2):
        first = slab_even if side == 1 else jnp.logical_not(slab_even)
        strip = jnp.where(first, got_a[PLANES], got_b[PLANES])
        for i in range(PLANES):
            ghost[side, i] = wide(jnp.where(first, got_a[i], got_b[i]), take_group(strip, i))

    for z in range(3, DEPTH - 3):
        for q in range(2):
            out[q, z] = u3[q, z]

    for side in range(2):
        z0, z1, z2 = (0, 1, 2) if side == 0 else (DEPTH - 1, DEPTH - 2, DEPTH - 3)
        a0, a1, a2 = [wide(kind[z].astype(jnp.float32), halo[G_TYPE + z]) for z in (z0, z1, z2)]
        v0, v1 = [wide(vel[z], halo[G_VEL + z]) for z in (z0, z1)]
        vg, ag = ghost[side, 10], ghost[side, 11]
        own_self = m_ref[9] * upper if side == 0 else m_ref[10] * lower
        for q in range(2):
            h = RATES[q]
            k0, k1, k2 = [wide(kappa[q, z], halo[G_KAPPA + q * DEPTH + z]) for z in (z0, z1, z2)]
            kg, kgg = ghost[side, 6 + q], ghost[side, 8 + q]
            k_face = 0.5 * (kg + k0)
            k01, k12, kg2 = 0.5 * (k0 + k1), 0.5 * (k1 + k2), 0.5 * (kg + kgg)
            c0 = [wide(conc[q, z0], halo[G_CONC + q * DEPTH + z0])]
            c0 += [edge_u[side, t, q] for t in range(2)]
            cg = [ghost[side, 2 * t + q] for t in range(3)]

            def drive(e, g, both):
                if side == 0:
                    to_e = scatter(m_ref, g)
                    to_g = gather(m_ref, e) if both else None
                else:
                    to_e = gather(m_ref, g)
                    to_g = scatter(m_ref, e) if both else None
                flow = k_face * (g - e)
                return a0 * (flow + h * to_e), (ag * (h * to_g - flow) if both else None)

            kx0, ky0 = face_x(k0), face_y(k0)
            e1, d1 = drive(c0[0], cg[0], True)
            f1, g1 = drive(c0[1] + e1, cg[1] + d1, True)
            ghost_self = m_ref[10] if side == 0 else m_ref[9]
            d2 = d1 + g1 + ag * (
                in_plane(d1, face_x(kg), face_y(kg), vg) - (kg2 + h * ghost_self) * d1
            )
            hold = k01 + h * own_self
            e2 = e1 + f1 + a0 * (in_plane(e1, kx0, ky0, v0) - hold * e1)
            n2 = a1 * (k01 * e1)
            f2, _ = drive(c0[2] + e2, cg[2] + d2, False)
            e3 = e2 + f2 + a0 * (in_plane(e2, kx0, ky0, v0) - hold * e2 + k01 * n2)
            n3 = n2 + a1 * (
                in_plane(n2, face_x(k1), face_y(k1), v1) - (k01 + k12) * n2 + k01 * e2
            )
            m3 = a2 * (k12 * n2)
            out[q, z0] = u3[q, z0] + e3[:, :COLS]
            out[q, z1] = u3[q, z1] + n3[:, :COLS]
            out[q, z2] = u3[q, z2] + m3[:, :COLS]


def swap(value, axis, parity):
    count = lax.axis_size(axis)
    pairs = []
    for i in range(parity, count - 1, 2):
        pairs += [(i, i + 1), (i + 1, i)]
    return lax.ppermute(value, axis, pairs)


def shape(*dims):
    return jax.ShapeDtypeStruct(dims, jnp.float32)


def call(kernel, outs, scratch=(), cost=2_000_000):
    return pl.pallas_call(
        kernel,
        out_shape=outs,
        scratch_shapes=list(scratch),
        cost_estimate=pl.CostEstimate(flops=cost, bytes_accessed=2_000_000, transcendentals=0),
        compiler_params=pltpu.CompilerParams(vmem_limit_bytes=40 * 2**20),
    )


def per_device(conc, kappa, velocity, cell_type, target_row, target_col, mortar_weight):
    faces = (target_row, target_col, mortar_weight)
    fields = (conc, kappa, velocity, cell_type)
    tile = (ROWS, COLS)
    wide_tile = (ROWS, WIDE)
    msg = call(pack_kernel, shape(TILES, *tile))(*fields, *faces)
    got_b = swap(msg, "stream", 1)
    got_a = swap(msg, "stream", 0)
    u3, msg_a, msg_b, halo, edge_u, m = call(
        block_kernel,
        (
            shape(2, DEPTH, *tile),
            shape(PLANES + 1, *tile),
            shape(PLANES + 1, *tile),
            shape(GROUPS, *tile),
            shape(2, 2, 2, *wide_tile),
            shape(11, *wide_tile),
        ),
        (
            pltpu.VMEM((2, 2, DEPTH + 2) + wide_tile, jnp.float32),
            pltpu.VMEM((2, DEPTH) + wide_tile, jnp.float32),
            pltpu.VMEM((2, DEPTH) + wide_tile, jnp.float32),
            pltpu.VMEM((2, DEPTH + 1) + wide_tile, jnp.float32),
            pltpu.VMEM((DEPTH,) + wide_tile, jnp.float32),
        ),
    )(*fields, *faces, got_a, got_b)
    side_b = swap(msg_b, "slab", 1)
    side_a = swap(msg_a, "slab", 0)
    return call(
        join_kernel,
        shape(2, DEPTH, *tile),
        (pltpu.VMEM((2, PLANES) + wide_tile, jnp.float32),),
    )(*fields, halo, edge_u, m, u3, side_a, side_b)


def solution(mesh):
    return jax.shard_map(
        per_device,
        mesh=mesh,
        in_specs=(
            P(None, "slab", None, "stream"),
            P(None, "slab", None, "stream"),
            P("slab", None, "stream"),
            P("slab", None, "stream"),
            P(None, None, "stream"),
            P(None, None, "stream"),
            P(None, None, "stream"),
        ),
        out_specs=P(None, "slab", None, "stream"),
        check_vma=False,
    )
```

```python
import jax
import jax.numpy as jnp
from jax import lax
from jax.experimental import pallas as pl
from jax.experimental.pallas import tpu as pltpu
from jax.sharding import PartitionSpec as P

RATES = (0.08, 0.12)
DEPTH, ROWS, COLS = 8, 64, 128
WIDE = 2 * COLS
HALO = 3
GROUP = 2 * HALO
SLOTS = COLS // GROUP
PLANES = 12
G_CONC, G_KAPPA, G_VEL, G_TYPE, G_FACE, GROUPS = 0, 16, 32, 40, 48, 54
TILES = -(-GROUPS // SLOTS)


def lanes_of(shape):
    return lax.broadcasted_iota(jnp.int32, shape, len(shape) - 1)


def edge_mask():
    lane = lanes_of((ROWS, COLS))
    return (lane < HALO) | (lane >= COLS - HALO)


def place_group(tile, plane, slot):
    lane = lanes_of(tile.shape)
    start = slot * GROUP
    moved = pltpu.roll(plane, (start + HALO) % COLS, 1)
    return jnp.where((lane >= start) & (lane < start + GROUP), moved, tile)


def take_group(tile, slot):
    moved = pltpu.roll(tile, (COLS - slot * GROUP - HALO) % COLS, 1)
    return jnp.where(edge_mask(), moved, 0.0)


def wide(main, halo):
    return jnp.concatenate([main, halo], axis=1)


def shift_cols(x, by):
    return pltpu.roll(x, (-by) % x.shape[1], 1)


def shift_rows(x, by):
    return pltpu.roll(x, (-by) % x.shape[0], 0)


def in_plane(c, kx, ky, v):
    s = kx * (shift_cols(c, 1) - c) - v * c
    f = ky * (shift_rows(c, 1) - c)
    return (s - shift_cols(s, -1)) + (f - shift_rows(f, -1))


def face_x(k):
    return 0.5 * (k + shift_cols(k, 1))


def face_y(k):
    row = lax.broadcasted_iota(jnp.int32, k.shape, 0)
    return jnp.where(row < ROWS - 1, 0.5 * (k + shift_rows(k, 1)), 0.0)


def gather(m_ref, bed):
    total = None
    for b in (-1, 0, 1):
        at_b = shift_cols(bed, b) if b else bed
        for a in (-1, 0, 1):
            term = m_ref[3 * (a + 1) + b + 1] * (shift_rows(at_b, a) if a else at_b)
            total = term if total is None else total + term
    return total


def scatter(m_ref, water):
    total = None
    for b in (-1, 0, 1):
        part = None
        for a in (-1, 0, 1):
            term = m_ref[3 * (a + 1) + b + 1]
            if water is not None:
                term = term * water
            term = shift_rows(term, -a) if a else term
            part = term if part is None else part + term
        part = shift_cols(part, -b) if b else part
        total = part if total is None else total + part
    return total


def face_planes(row_ref, col_ref, w_ref):
    start = lax.axis_index("stream") * COLS
    row = lax.broadcasted_iota(jnp.int32, (ROWS, COLS), 0)
    col = lanes_of((ROWS, COLS)) + start
    out = [(row_ref[k] - row).astype(jnp.float32) for k in range(2)]
    out += [(col_ref[k] - col).astype(jnp.float32) for k in range(2)]
    return out + [w_ref[k] for k in range(2)]


def pack_kernel(
    conc_in, kappa_in, vel_in, kind_in, row_in, col_in, w_in,
    msg, conc, kappa, vel, active, faces,
    kind, row, col, w, sems,
):
    moves = [(conc_in, conc), (kappa_in, kappa), (vel_in, vel), (kind_in, kind)]
    moves += [(row_in, row), (col_in, col), (w_in, w)]
    copies = [pltpu.make_async_copy(*move, sems.at[i]) for i, move in enumerate(moves)]
    for copy in copies:
        copy.start()
    tiles = [jnp.zeros((ROWS, COLS), jnp.float32) for _ in range(TILES)]

    def put(group, plane):
        t, slot = divmod(group, SLOTS)
        tiles[t] = place_group(tiles[t], plane, slot)

    for q in range(2):
        if q == 0:
            copies[0].wait()
        for z in range(DEPTH):
            put(G_CONC + q * DEPTH + z, conc[q, z])
    copies[1].wait()
    for q in range(2):
        for z in range(DEPTH):
            put(G_KAPPA + q * DEPTH + z, kappa[q, z])
    copies[2].wait()
    copies[3].wait()
    for z in range(DEPTH):
        put(G_VEL + z, vel[z])
        on = kind[z].astype(jnp.float32)
        active[z] = on
        put(G_TYPE + z, on)
    for copy in copies[4:]:
        copy.wait()
    for i, plane in enumerate(face_planes(row, col, w)):
        faces[i] = plane
        put(G_FACE + i, plane)
    for t in range(TILES):
        msg[t] = tiles[t]


def merged(got_a, got_b):
    even = lax.axis_index("stream") % 2 == 0
    low = lax.rem(lanes_of((ROWS, COLS)), GROUP) < HALO
    return [jnp.where(low == even, got_b[t], got_a[t]) for t in range(TILES)]


def slab_flags():
    slab = lax.axis_index("slab")
    upper = (slab > 0).astype(jnp.float32)
    lower = (slab < lax.axis_size("slab") - 1).astype(jnp.float32)
    return slab % 2 == 0, upper, lower


def layers_of(side):
    return (0, 1, 2) if side == 0 else (DEPTH - 1, DEPTH - 2, DEPTH - 3)


def edge_kernel(conc, kappa, vel, active, faces, got_a, got_b, msg_a, msg_b, edge_u, m_out):
    tiles = merged(got_a, got_b)

    def halo(group):
        t, slot = divmod(group, SLOTS)
        return take_group(tiles[t], slot)

    planes = [wide(faces[i], halo(G_FACE + i)) for i in range(6)]
    rows_hit = [[planes[k] == a for a in (-1, 0, 1)] for k in range(2)]
    for b in (-1, 0, 1):
        parts = [jnp.where(planes[2 + k] == b, planes[4 + k], 0.0) for k in range(2)]
        for a in (-1, 0, 1):
            m_out[3 * (a + 1) + b + 1] = jnp.where(rows_hit[0][a + 1], parts[0], 0.0) + jnp.where(
                rows_hit[1][a + 1], parts[1], 0.0
            )
    m_out[9] = scatter(m_out, None)
    m_out[10] = planes[4] + planes[5]
    slab_even, upper, lower = slab_flags()

    sent = []
    for side in range(2):
        z0, z1, z2 = layers_of(side)
        own = m_out[9] * upper if side == 0 else m_out[10] * lower
        a0, a1 = [wide(active[z], halo(G_TYPE + z)) for z in (z0, z1)]
        v0, v1 = [wide(vel[z], halo(G_VEL + z)) for z in (z0, z1)]
        rows = [None] * PLANES
        for q in range(2):
            k0, k1, k2 = [wide(kappa[q, z], halo(G_KAPPA + q * DEPTH + z)) for z in (z0, z1, z2)]
            c0, c1, c2 = [wide(conc[q, z], halo(G_CONC + q * DEPTH + z)) for z in (z0, z1, z2)]
            kx0, ky0 = face_x(k0), face_y(k0)
            k01, k12 = 0.5 * (k0 + k1), 0.5 * (k1 + k2)
            hold = RATES[q] * own
            u0 = c0 + a0 * (in_plane(c0, kx0, ky0, v0) + k01 * (c1 - c0) - hold * c0)
            edge_u[side, 0, q] = u0
            u1 = c1 + a1 * (
                in_plane(c1, face_x(k1), face_y(k1), v1) + k12 * (c2 - c1) - k01 * (c1 - c0)
            )
            w0 = u0 + a0 * (in_plane(u0, kx0, ky0, v0) + k01 * (u1 - u0) - hold * u0)
            edge_u[side, 1, q] = w0
            rows[q], rows[2 + q], rows[4 + q] = c0, u0, w0
            rows[6 + q], rows[8 + q] = k0, k1
        rows[10], rows[11] = v0, a0
        sent.append(rows)

    strip_a = jnp.zeros((ROWS, COLS), jnp.float32)
    strip_b = strip_a
    for i, (top, bottom) in enumerate(zip(*sent)):
        to_a, to_b = jnp.where(slab_even, bottom, top), jnp.where(slab_even, top, bottom)
        msg_a[i] = to_a[:, :COLS]
        msg_b[i] = to_b[:, :COLS]
        strip_a = place_group(strip_a, to_a[:, COLS:], i)
        strip_b = place_group(strip_b, to_b[:, COLS:], i)
    msg_a[PLANES] = strip_a
    msg_b[PLANES] = strip_b


def block_kernel(
    conc, kappa, vel, active, m_ref, got_a, got_b,
    u3, coef, av,
    halo, cells, kx, ky, kz, own,
):
    for t, tile in enumerate(merged(got_a, got_b)):
        for slot in range(min(SLOTS, G_FACE - t * SLOTS)):
            halo[t * SLOTS + slot] = take_group(tile, slot)
    _, upper, lower = slab_flags()
    own[...] = jnp.zeros(own.shape, jnp.float32)
    own[0] = m_ref[9] * upper
    own[DEPTH - 1] = m_ref[10] * lower

    def prepare(z, _):
        for q in range(2):
            k = wide(kappa[q, z], halo[G_KAPPA + q * DEPTH + z])
            kx[q, z] = face_x(k)
            ky[q, z] = face_y(k)
            cells[0, q, z + 1] = wide(conc[q, z], halo[G_CONC + q * DEPTH + z])
        return 0

    lax.fori_loop(0, DEPTH, prepare, 0)

    def prepare_z(z, _):
        for q in range(2):
            k = wide(kappa[q, z], halo[G_KAPPA + q * DEPTH + z])
            below = wide(kappa[q, z + 1], halo[G_KAPPA + q * DEPTH + z + 1])
            kz[q, z + 1] = 0.5 * (k + below)
        return 0

    lax.fori_loop(0, DEPTH - 1, prepare_z, 0)
    zeros = jnp.zeros((ROWS, WIDE), jnp.float32)
    for q in range(2):
        kz[q, 0] = zeros
        kz[q, DEPTH] = zeros
        for t in range(2):
            cells[t, q, 0] = zeros
            cells[t, q, DEPTH + 1] = zeros

    for side in range(2):
        z0, z1, z2 = layers_of(side)
        f01, f12 = (1, 2) if side == 0 else (DEPTH - 1, DEPTH - 2)
        for i, z in enumerate((z0, z1, z2)):
            av[side, i] = wide(active[z], halo[G_TYPE + z])
        for i, z in enumerate((z0, z1)):
            av[side, 3 + i] = wide(vel[z], halo[G_VEL + z])
        for q in range(2):
            c0 = cells[0, q, z0 + 1]
            items = [kx[q, z0], ky[q, z0], kx[q, z1], ky[q, z1], kz[q, f01], kz[q, f12]]
            items.append(kz[q, f01] + RATES[q] * own[z0])
            items.append(RATES[q] * (gather(m_ref, c0) if side == 0 else scatter(m_ref, c0)))
            items.append(wide(kappa[q, z0], halo[G_KAPPA + q * DEPTH + z0]))
            items.append(c0)
            for i, item in enumerate(items):
                coef[side, q, i] = item

    for step in range(3):
        now, later = step % 2, (step + 1) % 2

        def advance(z, _):
            a = wide(active[z], halo[G_TYPE + z])
            v = wide(vel[z], halo[G_VEL + z])
            for q in range(2):
                c = cells[now, q, z + 1]
                r = in_plane(c, kx[q, z], ky[q, z], v)
                r += kz[q, z + 1] * (cells[now, q, z + 2] - c)
                r -= kz[q, z] * (c - cells[now, q, z])
                r -= RATES[q] * own[z] * c
                new = c + a * r
                if step == 2:
                    u3[q, z] = new[:, :COLS]
                else:
                    cells[later, q, z + 1] = new
            return 0

        lax.fori_loop(0, DEPTH, advance, 0)


def join_kernel(coef, av, edge_u, m_ref, u3, got_a, got_b, out, ghost, result, sems):
    copies = []

    def send(q, z, count):
        part = pl.ds(z, count)
        copy = pltpu.make_async_copy(result.at[q, part], out.at[q, part], sems.at[len(copies)])
        copy.start()
        copies.append(copy)

    for q in range(2):
        for z in range(3, DEPTH - 3):
            result[q, z] = u3[q, z]
        send(q, 3, DEPTH - 6)
    slab_even, _, _ = slab_flags()
    for side in range(2):
        first = slab_even if side == 1 else jnp.logical_not(slab_even)
        strip = jnp.where(first, got_a[PLANES], got_b[PLANES])
        for i in range(PLANES):
            ghost[side, i] = wide(jnp.where(first, got_a[i], got_b[i]), take_group(strip, i))

    for side in range(2):
        z0, z1, z2 = layers_of(side)
        a0, a1, a2, v0, v1 = [av[side, i] for i in range(5)]
        vg, ag = ghost[side, 10], ghost[side, 11]
        for q in range(2):
            h = RATES[q]
            kx0, ky0, kx1, ky1, k01, k12, hold, first_to_g, k0, first_c = [
                coef[side, q, i] for i in range(10)
            ]
            kg, kgg = ghost[side, 6 + q], ghost[side, 8 + q]
            k_face, kg2 = 0.5 * (kg + k0), 0.5 * (kg + kgg)
            own_c = [first_c, edge_u[side, 0, q], edge_u[side, 1, q]]
            ghost_c = [ghost[side, 2 * t + q] for t in range(3)]
            to_lower, to_upper = (gather, scatter) if side == 0 else (scatter, gather)

            g, e = ghost_c[0], own_c[0]
            flow = k_face * (g - e)
            e1 = a0 * (flow + h * to_upper(m_ref, g))
            d1 = ag * (first_to_g - flow)
            g, e = ghost_c[1] + d1, own_c[1] + e1
            flow = k_face * (g - e)
            ghost_self = m_ref[10] if side == 0 else m_ref[9]
            d2 = d1 + ag * (
                in_plane(d1, face_x(kg), face_y(kg), vg)
                - (kg2 + h * ghost_self) * d1
                + (h * to_lower(m_ref, e) - flow)
            )
            e2 = e1 + a0 * (
                in_plane(e1, kx0, ky0, v0) - hold * e1 + (flow + h * to_upper(m_ref, g))
            )
            n2 = a1 * (k01 * e1)
            g, e = ghost_c[2] + d2, own_c[2] + e2
            flow = k_face * (g - e)
            e3 = e2 + a0 * (
                in_plane(e2, kx0, ky0, v0) - hold * e2 + k01 * n2
                + (flow + h * to_upper(m_ref, g))
            )
            n3 = n2 + a1 * (in_plane(n2, kx1, ky1, v1) - (k01 + k12) * n2 + k01 * e2)
            m3 = a2 * (k12 * n2)
            result[q, z0] = u3[q, z0] + e3[:, :COLS]
            result[q, z1] = u3[q, z1] + n3[:, :COLS]
            result[q, z2] = u3[q, z2] + m3[:, :COLS]
            send(q, min(z0, z2), 3)
    for copy in copies:
        copy.wait()


def swap(value, axis, parity):
    count = lax.axis_size(axis)
    pairs = []
    for i in range(parity, count - 1, 2):
        pairs += [(i, i + 1), (i + 1, i)]
    return lax.ppermute(value, axis, pairs)


def shape(*dims):
    return jax.ShapeDtypeStruct(dims, jnp.float32)


def call(kernel, outs, scratch=(), **specs):
    return pl.pallas_call(
        kernel,
        out_shape=outs,
        scratch_shapes=list(scratch),
        cost_estimate=pl.CostEstimate(flops=2**21, bytes_accessed=2**21, transcendentals=0),
        compiler_params=pltpu.CompilerParams(vmem_limit_bytes=40 * 2**20),
        **specs,
    )


def per_device(conc, kappa, velocity, cell_type, target_row, target_col, mortar_weight):
    tile = (ROWS, COLS)
    wide_tile = (ROWS, WIDE)
    faces = (2,) + tile
    msg, *fields, offsets = call(
        pack_kernel,
        (
            shape(TILES, *tile),
            shape(2, DEPTH, *tile),
            shape(2, DEPTH, *tile),
            shape(DEPTH, *tile),
            shape(DEPTH, *tile),
            shape(6, *tile),
        ),
        (
            pltpu.VMEM((DEPTH,) + tile, jnp.int32),
            pltpu.VMEM(faces, jnp.int32),
            pltpu.VMEM(faces, jnp.int32),
            pltpu.VMEM(faces, jnp.float32),
            pltpu.SemaphoreType.DMA((7,)),
        ),
        in_specs=[pl.BlockSpec(memory_space=pl.ANY)] * 7,
    )(
        *[
            pltpu.with_memory_space_constraint(x, pltpu.HBM)
            for x in (conc, kappa, velocity, cell_type, target_row, target_col, mortar_weight)
        ]
    )
    got_b = swap(msg, "stream", 1)
    got_a = swap(msg, "stream", 0)
    msg_a, msg_b, edge_u, m = call(
        edge_kernel,
        (
            shape(PLANES + 1, *tile),
            shape(PLANES + 1, *tile),
            shape(2, 2, 2, *wide_tile),
            shape(11, *wide_tile),
        ),
    )(*fields, offsets, got_a, got_b)
    side_b = swap(msg_b, "slab", 1)
    side_a = swap(msg_a, "slab", 0)
    u3, coef, av = call(
        block_kernel,
        (
            shape(2, DEPTH, *tile),
            shape(2, 2, 10, *wide_tile),
            shape(2, 5, *wide_tile),
        ),
        (
            pltpu.VMEM((G_FACE,) + tile, jnp.float32),
            pltpu.VMEM((2, 2, DEPTH + 2) + wide_tile, jnp.float32),
            pltpu.VMEM((2, DEPTH) + wide_tile, jnp.float32),
            pltpu.VMEM((2, DEPTH) + wide_tile, jnp.float32),
            pltpu.VMEM((2, DEPTH + 1) + wide_tile, jnp.float32),
            pltpu.VMEM((DEPTH,) + wide_tile, jnp.float32),
        ),
    )(*fields, m, got_a, got_b)
    return call(
        join_kernel,
        shape(2, DEPTH, *tile),
        (
            pltpu.VMEM((2, PLANES) + wide_tile, jnp.float32),
            pltpu.VMEM((2, DEPTH) + tile, jnp.float32),
            pltpu.SemaphoreType.DMA((6,)),
        ),
        out_specs=pl.BlockSpec(memory_space=pl.ANY),
    )(coef, av, edge_u, m, u3, side_a, side_b)


def solution(mesh):
    return jax.shard_map(
        per_device,
        mesh=mesh,
        in_specs=(
            P(None, "slab", None, "stream"),
            P(None, "slab", None, "stream"),
            P("slab", None, "stream"),
            P("slab", None, "stream"),
            P(None, None, "stream"),
            P(None, None, "stream"),
            P(None, None, "stream"),
        ),
        out_specs=P(None, "slab", None, "stream"),
        check_vma=False,
    )
```

```python
import jax
import jax.numpy as jnp
from jax import lax
from jax.experimental import pallas as pl
from jax.experimental.pallas import tpu as pltpu
from jax.sharding import PartitionSpec as P

RATES = (0.08, 0.12)
DEPTH, ROWS, COLS = 8, 64, 128
WIDE = 2 * COLS
HALO = 3
GROUP = 2 * HALO
SLOTS = COLS // GROUP
PLANES, RAW, LATE = 12, 8, 4
G_CONC, G_KAPPA, G_VEL, G_TYPE, G_FACE, GROUPS = 0, 16, 32, 40, 48, 54
TILES = -(-GROUPS // SLOTS)


def lanes_of(shape):
    return lax.broadcasted_iota(jnp.int32, shape, len(shape) - 1)


def edge_mask():
    lane = lanes_of((ROWS, COLS))
    return (lane < HALO) | (lane >= COLS - HALO)


def place_group(tile, plane, slot):
    lane = lanes_of(tile.shape)
    start = slot * GROUP
    moved = pltpu.roll(plane, (start + HALO) % COLS, 1)
    return jnp.where((lane >= start) & (lane < start + GROUP), moved, tile)


def take_group(tile, slot):
    moved = pltpu.roll(tile, (COLS - slot * GROUP - HALO) % COLS, 1)
    return jnp.where(edge_mask(), moved, 0.0)


def wide(main, halo):
    return jnp.concatenate([main, halo], axis=1)


def shift_cols(x, by):
    return pltpu.roll(x, (-by) % x.shape[1], 1)


def shift_rows(x, by):
    return pltpu.roll(x, (-by) % x.shape[0], 0)


def in_plane(c, kx, ky, v):
    s = kx * (shift_cols(c, 1) - c) - v * c
    f = ky * (shift_rows(c, 1) - c)
    return (s - shift_cols(s, -1)) + (f - shift_rows(f, -1))


def face_x(k):
    return 0.5 * (k + shift_cols(k, 1))


def face_y(k):
    row = lax.broadcasted_iota(jnp.int32, k.shape, 0)
    return jnp.where(row < ROWS - 1, 0.5 * (k + shift_rows(k, 1)), 0.0)


def gather(m_ref, bed):
    total = None
    for b in (-1, 0, 1):
        at_b = shift_cols(bed, b) if b else bed
        for a in (-1, 0, 1):
            term = m_ref[3 * (a + 1) + b + 1] * (shift_rows(at_b, a) if a else at_b)
            total = term if total is None else total + term
    return total


def scatter(m_ref, water):
    total = None
    for b in (-1, 0, 1):
        part = None
        for a in (-1, 0, 1):
            term = m_ref[3 * (a + 1) + b + 1]
            if water is not None:
                term = term * water
            term = shift_rows(term, -a) if a else term
            part = term if part is None else part + term
        part = shift_cols(part, -b) if b else part
        total = part if total is None else total + part
    return total


def face_planes(row_ref, col_ref, w_ref):
    start = lax.axis_index("stream") * COLS
    row = lax.broadcasted_iota(jnp.int32, (ROWS, COLS), 0)
    col = lanes_of((ROWS, COLS)) + start
    out = [(row_ref[k] - row).astype(jnp.float32) for k in range(2)]
    out += [(col_ref[k] - col).astype(jnp.float32) for k in range(2)]
    return out + [w_ref[k] for k in range(2)]


def pack_kernel(
    conc_in, kappa_in, vel_in, kind_in, row_in, col_in, w_in,
    msg, raw_a, raw_b, conc, kappa, vel, active, faces,
    kind, row, col, w, sems,
):
    moves = [(conc_in, conc), (kappa_in, kappa), (vel_in, vel), (kind_in, kind)]
    moves += [(row_in, row), (col_in, col), (w_in, w)]
    slab_even, _, _ = slab_flags()
    for raw, lower in ((raw_a, slab_even), (raw_b, jnp.logical_not(slab_even))):
        first = jnp.where(lower, DEPTH - 1, 0)
        second = jnp.where(lower, DEPTH - 2, 1)
        moves += [(conc_in.at[:, first], raw.at[0:2]), (kappa_in.at[:, first], raw.at[2:4])]
        moves += [(kappa_in.at[:, second], raw.at[4:6]), (vel_in.at[first], raw.at[6])]
    copies = [pltpu.make_async_copy(*move, sems.at[i]) for i, move in enumerate(moves)]
    for copy in copies:
        copy.start()
    tiles = [jnp.zeros((ROWS, COLS), jnp.float32) for _ in range(TILES)]

    def put(group, plane):
        t, slot = divmod(group, SLOTS)
        tiles[t] = place_group(tiles[t], plane, slot)

    for q in range(2):
        if q == 0:
            copies[0].wait()
        for z in range(DEPTH):
            put(G_CONC + q * DEPTH + z, conc[q, z])
    copies[1].wait()
    for q in range(2):
        for z in range(DEPTH):
            put(G_KAPPA + q * DEPTH + z, kappa[q, z])
    copies[2].wait()
    copies[3].wait()
    for z in range(DEPTH):
        put(G_VEL + z, vel[z])
        on = kind[z].astype(jnp.float32)
        active[z] = on
        put(G_TYPE + z, on)
    for raw, lower in ((raw_a, slab_even), (raw_b, jnp.logical_not(slab_even))):
        raw[7] = jnp.where(lower, active[DEPTH - 1], active[0])
    for copy in copies[4:]:
        copy.wait()
    for i, plane in enumerate(face_planes(row, col, w)):
        faces[i] = plane
        put(G_FACE + i, plane)
    for t in range(TILES):
        msg[t] = tiles[t]


def merged(got_a, got_b):
    even = lax.axis_index("stream") % 2 == 0
    low = lax.rem(lanes_of((ROWS, COLS)), GROUP) < HALO
    return [jnp.where(low == even, got_b[t], got_a[t]) for t in range(TILES)]


def slab_flags():
    slab = lax.axis_index("slab")
    upper = (slab > 0).astype(jnp.float32)
    lower = (slab < lax.axis_size("slab") - 1).astype(jnp.float32)
    return slab % 2 == 0, upper, lower


def layers_of(side):
    return (0, 1, 2) if side == 0 else (DEPTH - 1, DEPTH - 2, DEPTH - 3)


def edge_kernel(conc, kappa, vel, active, faces, got_a, got_b, msg_a, msg_b, edge_u, m_out):
    tiles = merged(got_a, got_b)

    def halo(group):
        t, slot = divmod(group, SLOTS)
        return take_group(tiles[t], slot)

    planes = [wide(faces[i], halo(G_FACE + i)) for i in range(6)]
    rows_hit = [[planes[k] == a for a in (-1, 0, 1)] for k in range(2)]
    for b in (-1, 0, 1):
        parts = [jnp.where(planes[2 + k] == b, planes[4 + k], 0.0) for k in range(2)]
        for a in (-1, 0, 1):
            m_out[3 * (a + 1) + b + 1] = jnp.where(rows_hit[0][a + 1], parts[0], 0.0) + jnp.where(
                rows_hit[1][a + 1], parts[1], 0.0
            )
    m_out[9] = scatter(m_out, None)
    m_out[10] = planes[4] + planes[5]
    slab_even, upper, lower = slab_flags()

    sent = []
    for side in range(2):
        z0, z1, z2 = layers_of(side)
        own = m_out[9] * upper if side == 0 else m_out[10] * lower
        a0, a1 = [wide(active[z], halo(G_TYPE + z)) for z in (z0, z1)]
        v0, v1 = [wide(vel[z], halo(G_VEL + z)) for z in (z0, z1)]
        rows = [None] * PLANES
        for q in range(2):
            k0, k1, k2 = [wide(kappa[q, z], halo(G_KAPPA + q * DEPTH + z)) for z in (z0, z1, z2)]
            c0, c1, c2 = [wide(conc[q, z], halo(G_CONC + q * DEPTH + z)) for z in (z0, z1, z2)]
            kx0, ky0 = face_x(k0), face_y(k0)
            k01, k12 = 0.5 * (k0 + k1), 0.5 * (k1 + k2)
            hold = RATES[q] * own
            u0 = c0 + a0 * (in_plane(c0, kx0, ky0, v0) + k01 * (c1 - c0) - hold * c0)
            edge_u[side, 0, q] = u0
            u1 = c1 + a1 * (
                in_plane(c1, face_x(k1), face_y(k1), v1) + k12 * (c2 - c1) - k01 * (c1 - c0)
            )
            w0 = u0 + a0 * (in_plane(u0, kx0, ky0, v0) + k01 * (u1 - u0) - hold * u0)
            edge_u[side, 1, q] = w0
            rows[q], rows[2 + q], rows[4 + q] = c0, k0, k1
            rows[RAW + q], rows[RAW + 2 + q] = u0, w0
        rows[6], rows[7] = v0, a0
        sent.append(rows)

    strip_a = jnp.zeros((ROWS, COLS), jnp.float32)
    strip_b = strip_a
    for i, (top, bottom) in enumerate(zip(*sent)):
        to_a, to_b = jnp.where(slab_even, bottom, top), jnp.where(slab_even, top, bottom)
        if i >= RAW:
            msg_a[i - RAW] = to_a[:, :COLS]
            msg_b[i - RAW] = to_b[:, :COLS]
        strip_a = place_group(strip_a, to_a[:, COLS:], i)
        strip_b = place_group(strip_b, to_b[:, COLS:], i)
    msg_a[LATE] = strip_a
    msg_b[LATE] = strip_b


def block_kernel(
    conc, kappa, vel, active, m_ref, got_a, got_b,
    u3, coef, av,
    halo, cells, kx, ky, kz, own,
):
    for t, tile in enumerate(merged(got_a, got_b)):
        for slot in range(min(SLOTS, G_FACE - t * SLOTS)):
            halo[t * SLOTS + slot] = take_group(tile, slot)
    _, upper, lower = slab_flags()
    own[...] = jnp.zeros(own.shape, jnp.float32)
    own[0] = m_ref[9] * upper
    own[DEPTH - 1] = m_ref[10] * lower

    def prepare(z, _):
        for q in range(2):
            k = wide(kappa[q, z], halo[G_KAPPA + q * DEPTH + z])
            kx[q, z] = face_x(k)
            ky[q, z] = face_y(k)
            cells[0, q, z + 1] = wide(conc[q, z], halo[G_CONC + q * DEPTH + z])
        return 0

    lax.fori_loop(0, DEPTH, prepare, 0)

    def prepare_z(z, _):
        for q in range(2):
            k = wide(kappa[q, z], halo[G_KAPPA + q * DEPTH + z])
            below = wide(kappa[q, z + 1], halo[G_KAPPA + q * DEPTH + z + 1])
            kz[q, z + 1] = 0.5 * (k + below)
        return 0

    lax.fori_loop(0, DEPTH - 1, prepare_z, 0)
    zeros = jnp.zeros((ROWS, WIDE), jnp.float32)
    for q in range(2):
        kz[q, 0] = zeros
        kz[q, DEPTH] = zeros
        for t in range(2):
            cells[t, q, 0] = zeros
            cells[t, q, DEPTH + 1] = zeros

    for side in range(2):
        z0, z1, z2 = layers_of(side)
        f01, f12 = (1, 2) if side == 0 else (DEPTH - 1, DEPTH - 2)
        for i, z in enumerate((z0, z1, z2)):
            av[side, i] = wide(active[z], halo[G_TYPE + z])
        for i, z in enumerate((z0, z1)):
            av[side, 3 + i] = wide(vel[z], halo[G_VEL + z])
        for q in range(2):
            c0 = cells[0, q, z0 + 1]
            items = [kx[q, z0], ky[q, z0], kx[q, z1], ky[q, z1], kz[q, f01], kz[q, f12]]
            items.append(kz[q, f01] + RATES[q] * own[z0])
            items.append(RATES[q] * (gather(m_ref, c0) if side == 0 else scatter(m_ref, c0)))
            items.append(wide(kappa[q, z0], halo[G_KAPPA + q * DEPTH + z0]))
            items.append(c0)
            for i, item in enumerate(items):
                coef[side, q, i] = item

    for step in range(3):
        now, later = step % 2, (step + 1) % 2

        def advance(z, _):
            a = wide(active[z], halo[G_TYPE + z])
            v = wide(vel[z], halo[G_VEL + z])
            for q in range(2):
                c = cells[now, q, z + 1]
                r = in_plane(c, kx[q, z], ky[q, z], v)
                r += kz[q, z + 1] * (cells[now, q, z + 2] - c)
                r -= kz[q, z] * (c - cells[now, q, z])
                r -= RATES[q] * own[z] * c
                new = c + a * r
                if step == 2:
                    u3[q, z] = new[:, :COLS]
                else:
                    cells[later, q, z + 1] = new
            return 0

        lax.fori_loop(0, DEPTH, advance, 0)


def join_kernel(coef, av, edge_u, m_ref, u3, raw_a, raw_b, got_a, got_b, out, ghost, result, sems):
    copies = []

    def send(q, z, count):
        part = pl.ds(z, count)
        copy = pltpu.make_async_copy(result.at[q, part], out.at[q, part], sems.at[len(copies)])
        copy.start()
        copies.append(copy)

    for q in range(2):
        for z in range(3, DEPTH - 3):
            result[q, z] = u3[q, z]
        send(q, 3, DEPTH - 6)
    slab_even, _, _ = slab_flags()
    for side in range(2):
        first = slab_even if side == 1 else jnp.logical_not(slab_even)
        strip = jnp.where(first, got_a[LATE], got_b[LATE])
        for i in range(PLANES):
            from_a, from_b = (raw_a[i], raw_b[i]) if i < RAW else (got_a[i - RAW], got_b[i - RAW])
            ghost[side, i] = wide(jnp.where(first, from_a, from_b), take_group(strip, i))

    for side in range(2):
        z0, z1, z2 = layers_of(side)
        a0, a1, a2, v0, v1 = [av[side, i] for i in range(5)]
        vg, ag = ghost[side, 6], ghost[side, 7]
        for q in range(2):
            h = RATES[q]
            kx0, ky0, kx1, ky1, k01, k12, hold, first_to_g, k0, first_c = [
                coef[side, q, i] for i in range(10)
            ]
            kg, kgg = ghost[side, 2 + q], ghost[side, 4 + q]
            k_face, kg2 = 0.5 * (kg + k0), 0.5 * (kg + kgg)
            own_c = [first_c, edge_u[side, 0, q], edge_u[side, 1, q]]
            ghost_c = [ghost[side, i + q] for i in (0, RAW, RAW + 2)]
            to_lower, to_upper = (gather, scatter) if side == 0 else (scatter, gather)

            g, e = ghost_c[0], own_c[0]
            flow = k_face * (g - e)
            e1 = a0 * (flow + h * to_upper(m_ref, g))
            d1 = ag * (first_to_g - flow)
            g, e = ghost_c[1] + d1, own_c[1] + e1
            flow = k_face * (g - e)
            ghost_self = m_ref[10] if side == 0 else m_ref[9]
            d2 = d1 + ag * (
                in_plane(d1, face_x(kg), face_y(kg), vg)
                - (kg2 + h * ghost_self) * d1
                + (h * to_lower(m_ref, e) - flow)
            )
            e2 = e1 + a0 * (
                in_plane(e1, kx0, ky0, v0) - hold * e1 + (flow + h * to_upper(m_ref, g))
            )
            n2 = a1 * (k01 * e1)
            g, e = ghost_c[2] + d2, own_c[2] + e2
            flow = k_face * (g - e)
            e3 = e2 + a0 * (
                in_plane(e2, kx0, ky0, v0) - hold * e2 + k01 * n2
                + (flow + h * to_upper(m_ref, g))
            )
            n3 = n2 + a1 * (in_plane(n2, kx1, ky1, v1) - (k01 + k12) * n2 + k01 * e2)
            m3 = a2 * (k12 * n2)
            result[q, z0] = u3[q, z0] + e3[:, :COLS]
            result[q, z1] = u3[q, z1] + n3[:, :COLS]
            result[q, z2] = u3[q, z2] + m3[:, :COLS]
            send(q, min(z0, z2), 3)
    for copy in copies:
        copy.wait()


def swap(value, axis, parity):
    count = lax.axis_size(axis)
    pairs = []
    for i in range(parity, count - 1, 2):
        pairs += [(i, i + 1), (i + 1, i)]
    return lax.ppermute(value, axis, pairs)


def shape(*dims):
    return jax.ShapeDtypeStruct(dims, jnp.float32)


def call(kernel, outs, scratch=(), **specs):
    return pl.pallas_call(
        kernel,
        out_shape=outs,
        scratch_shapes=list(scratch),
        cost_estimate=pl.CostEstimate(flops=2**21, bytes_accessed=2**21, transcendentals=0),
        compiler_params=pltpu.CompilerParams(vmem_limit_bytes=40 * 2**20),
        **specs,
    )


def per_device(conc, kappa, velocity, cell_type, target_row, target_col, mortar_weight):
    tile = (ROWS, COLS)
    wide_tile = (ROWS, WIDE)
    faces = (2,) + tile
    msg, raw_a, raw_b, *fields, offsets = call(
        pack_kernel,
        (
            shape(TILES, *tile),
            shape(RAW, *tile),
            shape(RAW, *tile),
            shape(2, DEPTH, *tile),
            shape(2, DEPTH, *tile),
            shape(DEPTH, *tile),
            shape(DEPTH, *tile),
            shape(6, *tile),
        ),
        (
            pltpu.VMEM((DEPTH,) + tile, jnp.int32),
            pltpu.VMEM(faces, jnp.int32),
            pltpu.VMEM(faces, jnp.int32),
            pltpu.VMEM(faces, jnp.float32),
            pltpu.SemaphoreType.DMA((15,)),
        ),
        in_specs=[pl.BlockSpec(memory_space=pl.ANY)] * 7,
    )(
        *[
            pltpu.with_memory_space_constraint(x, pltpu.HBM)
            for x in (conc, kappa, velocity, cell_type, target_row, target_col, mortar_weight)
        ]
    )
    got_b = swap(msg, "stream", 1)
    got_a = swap(msg, "stream", 0)
    raw_b = swap(raw_b, "slab", 1)
    raw_a = swap(raw_a, "slab", 0)
    msg_a, msg_b, edge_u, m = call(
        edge_kernel,
        (
            shape(LATE + 1, *tile),
            shape(LATE + 1, *tile),
            shape(2, 2, 2, *wide_tile),
            shape(11, *wide_tile),
        ),
    )(*fields, offsets, got_a, got_b)
    side_b = swap(msg_b, "slab", 1)
    side_a = swap(msg_a, "slab", 0)
    u3, coef, av = call(
        block_kernel,
        (
            shape(2, DEPTH, *tile),
            shape(2, 2, 10, *wide_tile),
            shape(2, 5, *wide_tile),
        ),
        (
            pltpu.VMEM((G_FACE,) + tile, jnp.float32),
            pltpu.VMEM((2, 2, DEPTH + 2) + wide_tile, jnp.float32),
            pltpu.VMEM((2, DEPTH) + wide_tile, jnp.float32),
            pltpu.VMEM((2, DEPTH) + wide_tile, jnp.float32),
            pltpu.VMEM((2, DEPTH + 1) + wide_tile, jnp.float32),
            pltpu.VMEM((DEPTH,) + wide_tile, jnp.float32),
        ),
    )(*fields, m, got_a, got_b)
    return call(
        join_kernel,
        shape(2, DEPTH, *tile),
        (
            pltpu.VMEM((2, PLANES) + wide_tile, jnp.float32),
            pltpu.VMEM((2, DEPTH) + tile, jnp.float32),
            pltpu.SemaphoreType.DMA((6,)),
        ),
        out_specs=pl.BlockSpec(memory_space=pl.ANY),
    )(coef, av, edge_u, m, u3, raw_a, raw_b, side_a, side_b)


def solution(mesh):
    return jax.shard_map(
        per_device,
        mesh=mesh,
        in_specs=(
            P(None, "slab", None, "stream"),
            P(None, "slab", None, "stream"),
            P("slab", None, "stream"),
            P("slab", None, "stream"),
            P(None, None, "stream"),
            P(None, None, "stream"),
            P(None, None, "stream"),
        ),
        out_specs=P(None, "slab", None, "stream"),
        check_vma=False,
    )
```

```python
import jax
import jax.numpy as jnp
from jax import lax
from jax.experimental import pallas as pl
from jax.experimental.pallas import tpu as pltpu
from jax.sharding import PartitionSpec as P

RATES = (0.08, 0.12)
DEPTH, ROWS, COLS = 8, 64, 128
LANES = 2 * ROWS
EDGE = 8
TALL = COLS + 2 * EDGE
G_CONC, G_KAPPA, G_VT, G_FACE, GROUPS = 0, 8, 16, 24, 27
RAW = 4
LATE = 2 * TALL + RAW * 2 * EDGE


def first_half(shape):
    return lax.broadcasted_iota(jnp.int32, shape, 1) < ROWS


def halves(x, y):
    return jnp.where(first_half(x.shape), x, y)


def doubled(x):
    other = pltpu.roll(x, ROWS, 1)
    return halves(x, other), halves(other, x)


def shift_cols(x, by):
    return pltpu.roll(x, (-by) % x.shape[0], 0)


def shift_rows(x, by):
    return pltpu.roll(x, (-by) % LANES, 1)


def in_plane(c, kx, ky, v):
    s = kx * (shift_cols(c, 1) - c) - v * c
    f = ky * (shift_rows(c, 1) - c)
    return (s - shift_cols(s, -1)) + (f - shift_rows(f, -1))


def face_x(k):
    return 0.5 * (k + shift_cols(k, 1))


def face_y(k):
    row = lax.rem(lax.broadcasted_iota(jnp.int32, k.shape, 1), ROWS)
    return jnp.where(row < ROWS - 1, 0.5 * (k + shift_rows(k, 1)), 0.0)


def gather(m_ref, bed):
    total = None
    for a in (-1, 0, 1):
        at_a = shift_rows(bed, a) if a else bed
        for b in (-1, 0, 1):
            term = m_ref[3 * (a + 1) + b + 1] * (shift_cols(at_a, b) if b else at_a)
            total = term if total is None else total + term
    return total


def scatter(m_ref, water):
    total = None
    for a in (-1, 0, 1):
        part = None
        for b in (-1, 0, 1):
            term = m_ref[3 * (a + 1) + b + 1]
            if water is not None:
                term = term * water
            term = shift_cols(term, -b) if b else term
            part = term if part is None else part + term
        part = shift_rows(part, -a) if a else part
        total = part if total is None else total + part
    return total


def slab_flags():
    slab = lax.axis_index("slab")
    upper = (slab > 0).astype(jnp.float32)
    lower = (slab < lax.axis_size("slab") - 1).astype(jnp.float32)
    return slab % 2 == 0, upper, lower


def stream_even():
    return lax.axis_index("stream") % 2 == 0


def layers_of(side):
    return (0, 1, 2) if side == 0 else (DEPTH - 1, DEPTH - 2, DEPTH - 3)


def pack_kernel(
    conc_in, kappa_in, vel_in, kind_in, row_in, col_in, w_in,
    msg_a, msg_b, raw_a, raw_b, conc, kappa, vel, active, faces,
    conc_s, kappa_s, vel_s, kind_s, row_s, col_s, w_s, sems,
):
    moves = [(conc_in, conc_s), (kappa_in, kappa_s), (vel_in, vel_s), (kind_in, kind_s)]
    moves += [(row_in, row_s), (col_in, col_s), (w_in, w_s)]
    copies = [pltpu.make_async_copy(*move, sems.at[i]) for i, move in enumerate(moves)]
    for copy in copies:
        copy.start()
    even = stream_even()
    slab_even, _, _ = slab_flags()

    def turned(first, second):
        return jnp.concatenate([first, second], axis=0).T

    def put(group, plane):
        head, tail = plane[:EDGE], plane[COLS - EDGE :]
        msg_a[group] = jnp.where(even, tail, head)
        msg_b[group] = jnp.where(even, head, tail)

    def put_raw(i, top, bottom):
        raw_a[i] = jnp.where(slab_even, bottom, top)
        raw_b[i] = jnp.where(slab_even, top, bottom)

    copies[0].wait()
    for z in range(DEPTH):
        conc[z] = turned(conc_s[0, z], conc_s[1, z])
        put(G_CONC + z, conc[z])
    copies[1].wait()
    for z in range(DEPTH):
        kappa[z] = turned(kappa_s[0, z], kappa_s[1, z])
        put(G_KAPPA + z, kappa[z])
    copies[2].wait()
    copies[3].wait()
    for z in range(DEPTH):
        on = kind_s[z].astype(jnp.float32)
        vel[z] = turned(vel_s[z], vel_s[z])
        active[z] = turned(on, on)
        put(G_VT + z, halves(vel[z], active[z]))
    for copy in copies[4:]:
        copy.wait()
    row = lax.broadcasted_iota(jnp.int32, (ROWS, COLS), 0)
    col = lax.broadcasted_iota(jnp.int32, (ROWS, COLS), 1) + lax.axis_index("stream") * COLS
    for k in range(2):
        offsets = (row_s[k] - row).astype(jnp.float32), (col_s[k] - col).astype(jnp.float32)
        for i, item in enumerate(offsets + (w_s[k],)):
            faces[2 * i + k] = turned(item, item)
    for i in range(3):
        put(G_FACE + i, halves(faces[2 * i], faces[2 * i + 1]))
    last = DEPTH - 1
    put_raw(0, conc[0], conc[last])
    put_raw(1, kappa[0], kappa[last])
    put_raw(2, kappa[1], kappa[last - 1])
    put_raw(3, halves(vel[0], active[0]), halves(vel[last], active[last]))


class Halo:
    def __init__(self, got_a, got_b):
        self.got = got_a, got_b
        self.even = stream_even()

    def sides(self, group):
        a, b = self.got[0][group], self.got[1][group]
        return jnp.where(self.even, b, a), jnp.where(self.even, a, b)

    def plane(self, ref, z, group):
        left, right = self.sides(group + z)
        return jnp.concatenate([left, ref[z], right], axis=0)

    def pair(self, refs, places, group):
        left, right = [doubled(x) for x in self.sides(group)]
        return [
            jnp.concatenate([left[i], refs[i][places[i]], right[i]], axis=0) for i in range(2)
        ]

    def motion(self, vel, active, z):
        return self.pair((vel, active), (z, z), G_VT + z)


def edge_kernel(conc, kappa, vel, active, faces, got_a, got_b, msg_a, msg_b, edge_u, m_out):
    halo = Halo(got_a, got_b)
    planes = [halo.pair((faces, faces), (2 * i, 2 * i + 1), G_FACE + i) for i in range(3)]
    rate = jnp.where(first_half((TALL, LANES)), RATES[0], RATES[1])
    weights = [rate * planes[2][k] for k in range(2)]
    for a in (-1, 0, 1):
        parts = [jnp.where(planes[0][k] == a, weights[k], 0.0) for k in range(2)]
        for b in (-1, 0, 1):
            hits = [jnp.where(planes[1][k] == b, parts[k], 0.0) for k in range(2)]
            m_out[3 * (a + 1) + b + 1] = hits[0] + hits[1]
    m_out[9] = scatter(m_out, None)
    m_out[10] = weights[0] + weights[1]
    slab_even, upper, lower = slab_flags()

    sent = []
    for side in range(2):
        z0, z1, z2 = layers_of(side)
        hold = m_out[9] * upper if side == 0 else m_out[10] * lower
        (v0, a0), (v1, a1) = [halo.motion(vel, active, z) for z in (z0, z1)]
        k0, k1, k2 = [halo.plane(kappa, z, G_KAPPA) for z in (z0, z1, z2)]
        c0, c1, c2 = [halo.plane(conc, z, G_CONC) for z in (z0, z1, z2)]
        kx0, ky0 = face_x(k0), face_y(k0)
        k01, k12 = 0.5 * (k0 + k1), 0.5 * (k1 + k2)
        flow = k01 * (c1 - c0)
        u0 = c0 + a0 * (in_plane(c0, kx0, ky0, v0) + flow - hold * c0)
        edge_u[side, 0] = u0
        u1 = c1 + a1 * (in_plane(c1, face_x(k1), face_y(k1), v1) + k12 * (c2 - c1) - flow)
        w0 = u0 + a0 * (in_plane(u0, kx0, ky0, v0) + k01 * (u1 - u0) - hold * u0)
        edge_u[side, 1] = w0
        sent.append((u0, w0, c0, k0, k1, halves(v0, a0)))

    for i, (top, bottom) in enumerate(zip(*sent)):
        for msg, low in ((msg_a, slab_even), (msg_b, jnp.logical_not(slab_even))):
            if i < 2:
                msg[pl.ds(i * TALL, TALL)] = jnp.where(low, bottom, top)
            else:
                start = 2 * TALL + (i - 2) * 2 * EDGE
                msg[pl.ds(start, EDGE)] = jnp.where(low, bottom[:EDGE], top[:EDGE])
                msg[pl.ds(start + EDGE, EDGE)] = jnp.where(
                    low, bottom[TALL - EDGE :], top[TALL - EDGE :]
                )


def block_kernel(
    conc, kappa, vel, active, m_ref, got_a, got_b,
    u3, middle, coef, av,
    cells, kx, ky, kz, own, move, on,
):
    halo = Halo(got_a, got_b)
    _, upper, lower = slab_flags()
    zeros = jnp.zeros((TALL, LANES), jnp.float32)
    for z in range(1, DEPTH - 1):
        own[z] = zeros
    own[0] = m_ref[9] * upper
    own[DEPTH - 1] = m_ref[10] * lower
    above = None
    for z in range(DEPTH):
        k = halo.plane(kappa, z, G_KAPPA)
        kx[z] = face_x(k)
        ky[z] = face_y(k)
        kz[z] = zeros if above is None else 0.5 * (above + k)
        above = k
        cells[0, z + 1] = halo.plane(conc, z, G_CONC)
        move[z], on[z] = halo.motion(vel, active, z)
    kz[DEPTH] = zeros
    for t in range(2):
        cells[t, 0] = zeros
        cells[t, DEPTH + 1] = zeros

    for side in range(2):
        z0, z1, z2 = layers_of(side)
        f01, f12 = (1, 2) if side == 0 else (DEPTH - 1, DEPTH - 2)
        for i, z in enumerate((z0, z1, z2)):
            av[side, i] = on[z]
        for i, z in enumerate((z0, z1)):
            av[side, 3 + i] = move[z]
        c0 = cells[0, z0 + 1]
        items = [kx[z0], ky[z0], kx[z1], ky[z1], kz[f01], kz[f12], kz[f01] + own[z0]]
        items.append(gather(m_ref, c0) if side == 0 else scatter(m_ref, c0))
        items += [halo.plane(kappa, z0, G_KAPPA), c0]
        for i, item in enumerate(items):
            coef[side, i] = item

    for step in range(3):
        now, later = step % 2, (step + 1) % 2

        def advance(z, _):
            c = cells[now, z + 1]
            r = in_plane(c, kx[z], ky[z], move[z])
            r += kz[z + 1] * (cells[now, z + 2] - c) - kz[z] * (c - cells[now, z]) - own[z] * c
            new = c + on[z] * r
            if step == 2:
                u3[z] = new[EDGE : EDGE + COLS]
            else:
                cells[later, z + 1] = new
            return 0

        lax.fori_loop(0, DEPTH, advance, 0)
    for z in range(3, DEPTH - 3):
        back = u3[z].T
        middle[0, z - 3] = back[:ROWS]
        middle[1, z - 3] = back[ROWS:]


def join_kernel(
    coef, av, edge_u, m_ref, u3, middle, raw_a, raw_b, got_a, got_b, out, ghost, result, sems
):
    copies = []

    def send(source, z, count):
        target = out.at[:, pl.ds(z, count)]
        copies.append(pltpu.make_async_copy(source, target, sems.at[len(copies)]))
        copies[-1].start()

    send(middle, 3, DEPTH - 6)
    slab_even, _, _ = slab_flags()
    for side in range(2):
        first = slab_even if side == 1 else jnp.logical_not(slab_even)
        for i in range(2):
            part = pl.ds(i * TALL, TALL)
            ghost[side, i] = jnp.where(first, got_a[part], got_b[part])
        for i in range(RAW):
            left = pl.ds(2 * TALL + i * 2 * EDGE, EDGE)
            right = pl.ds(2 * TALL + i * 2 * EDGE + EDGE, EDGE)
            ghost[side, 2 + i, pl.ds(0, EDGE)] = jnp.where(first, got_a[left], got_b[left])
            ghost[side, 2 + i, pl.ds(EDGE, COLS)] = jnp.where(first, raw_a[i], raw_b[i])
            ghost[side, 2 + i, pl.ds(EDGE + COLS, EDGE)] = jnp.where(
                first, got_a[right], got_b[right]
            )

    for side in range(2):
        z0, z1, z2 = layers_of(side)
        a0, a1, a2, v0, v1 = [av[side, i] for i in range(5)]
        kx0, ky0, kx1, ky1, k01, k12, hold, first_to_g, k0, first_c = [
            coef[side, i] for i in range(10)
        ]
        kg, kgg = ghost[side, 3], ghost[side, 4]
        vg, ag = doubled(ghost[side, 5])
        k_face, kg2 = 0.5 * (kg + k0), 0.5 * (kg + kgg)
        own_c = [first_c, edge_u[side, 0], edge_u[side, 1]]
        ghost_c = [ghost[side, i] for i in (2, 0, 1)]
        to_lower, to_upper = (gather, scatter) if side == 0 else (scatter, gather)

        g, e = ghost_c[0], own_c[0]
        flow = k_face * (g - e)
        e1 = a0 * (flow + to_upper(m_ref, g))
        d1 = ag * (first_to_g - flow)
        g, e = ghost_c[1] + d1, own_c[1] + e1
        flow = k_face * (g - e)
        ghost_self = m_ref[10] if side == 0 else m_ref[9]
        d2 = d1 + ag * (
            in_plane(d1, face_x(kg), face_y(kg), vg)
            - (kg2 + ghost_self) * d1
            + (to_lower(m_ref, e) - flow)
        )
        e2 = e1 + a0 * (in_plane(e1, kx0, ky0, v0) - hold * e1 + (flow + to_upper(m_ref, g)))
        n2 = a1 * (k01 * e1)
        g, e = ghost_c[2] + d2, own_c[2] + e2
        flow = k_face * (g - e)
        e3 = e2 + a0 * (
            in_plane(e2, kx0, ky0, v0) - hold * e2 + k01 * n2 + (flow + to_upper(m_ref, g))
        )
        n3 = n2 + a1 * (in_plane(n2, kx1, ky1, v1) - (k01 + k12) * n2 + k01 * e2)
        m3 = a2 * (k12 * n2)
        low = min(z0, z2)
        for z, x in ((z0, e3), (z1, n3), (z2, m3)):
            back = (u3[z] + x[EDGE : EDGE + COLS]).T
            result[side, 0, z - low] = back[:ROWS]
            result[side, 1, z - low] = back[ROWS:]
        send(result.at[side], low, 3)
    for copy in copies:
        copy.wait()


def swap(value, axis, parity):
    count = lax.axis_size(axis)
    pairs = []
    for i in range(parity, count - 1, 2):
        pairs += [(i, i + 1), (i + 1, i)]
    return lax.ppermute(value, axis, pairs)


def shape(*dims):
    return jax.ShapeDtypeStruct(dims, jnp.float32)


def call(kernel, outs, scratch=(), **specs):
    return pl.pallas_call(
        kernel,
        out_shape=outs,
        scratch_shapes=list(scratch),
        cost_estimate=pl.CostEstimate(flops=2**21, bytes_accessed=2**21, transcendentals=0),
        compiler_params=pltpu.CompilerParams(vmem_limit_bytes=40 * 2**20),
        **specs,
    )


def per_device(conc, kappa, velocity, cell_type, target_row, target_col, mortar_weight):
    tile = (ROWS, COLS)
    plane = (COLS, LANES)
    tall = (TALL, LANES)
    messages = [shape(GROUPS, EDGE, LANES)] * 2 + [shape(RAW, *plane)] * 2
    msg_a, msg_b, raw_a, raw_b, *fields, faces = call(
        pack_kernel,
        messages + [shape(DEPTH, *plane)] * 4 + [shape(6, *plane)],
        (
            pltpu.VMEM((2, DEPTH) + tile, jnp.float32),
            pltpu.VMEM((2, DEPTH) + tile, jnp.float32),
            pltpu.VMEM((DEPTH,) + tile, jnp.float32),
            pltpu.VMEM((DEPTH,) + tile, jnp.int32),
            pltpu.VMEM((2,) + tile, jnp.int32),
            pltpu.VMEM((2,) + tile, jnp.int32),
            pltpu.VMEM((2,) + tile, jnp.float32),
            pltpu.SemaphoreType.DMA((7,)),
        ),
        in_specs=[pl.BlockSpec(memory_space=pl.ANY)] * 7,
    )(
        *[
            pltpu.with_memory_space_constraint(x, pltpu.HBM)
            for x in (conc, kappa, velocity, cell_type, target_row, target_col, mortar_weight)
        ]
    )
    got_b = swap(msg_b, "stream", 1)
    got_a = swap(msg_a, "stream", 0)
    raw_b = swap(raw_b, "slab", 1)
    raw_a = swap(raw_a, "slab", 0)
    late_a, late_b, edge_u, m = call(
        edge_kernel,
        (shape(LATE, LANES), shape(LATE, LANES), shape(2, 2, *tall), shape(11, *tall)),
    )(*fields, faces, got_a, got_b)
    late_b = swap(late_b, "slab", 1)
    late_a = swap(late_a, "slab", 0)
    u3, middle, coef, av = call(
        block_kernel,
        (
            shape(DEPTH, *plane),
            shape(2, DEPTH - 6, *tile),
            shape(2, 10, *tall),
            shape(2, 5, *tall),
        ),
        (
            pltpu.VMEM((2, DEPTH + 2) + tall, jnp.float32),
            pltpu.VMEM((DEPTH,) + tall, jnp.float32),
            pltpu.VMEM((DEPTH,) + tall, jnp.float32),
            pltpu.VMEM((DEPTH + 1,) + tall, jnp.float32),
            pltpu.VMEM((DEPTH,) + tall, jnp.float32),
            pltpu.VMEM((DEPTH,) + tall, jnp.float32),
            pltpu.VMEM((DEPTH,) + tall, jnp.float32),
        ),
    )(*fields, m, got_a, got_b)
    return call(
        join_kernel,
        shape(2, DEPTH, *tile),
        (
            pltpu.VMEM((2, 2 + RAW) + tall, jnp.float32),
            pltpu.VMEM((2, 2, 3) + tile, jnp.float32),
            pltpu.SemaphoreType.DMA((3,)),
        ),
        out_specs=pl.BlockSpec(memory_space=pl.ANY),
    )(coef, av, edge_u, m, u3, middle, raw_a, raw_b, late_a, late_b)


def solution(mesh):
    return jax.shard_map(
        per_device,
        mesh=mesh,
        in_specs=(
            P(None, "slab", None, "stream"),
            P(None, "slab", None, "stream"),
            P("slab", None, "stream"),
            P("slab", None, "stream"),
            P(None, None, "stream"),
            P(None, None, "stream"),
            P(None, None, "stream"),
        ),
        out_specs=P(None, "slab", None, "stream"),
        check_vma=False,
    )
```

```python
import functools

import jax
import jax.numpy as jnp
from jax import lax
from jax.experimental import pallas as pl
from jax.experimental.pallas import tpu as pltpu
from jax.sharding import PartitionSpec as P

RATES = (0.08, 0.12)
DEPTH, ROWS, COLS = 8, 64, 128
LANES = 2 * ROWS
EDGE = 8
TALL = COLS + 2 * EDGE
G_CONC, G_KAPPA, G_VT, G_FACE, GROUPS = 0, 8, 16, 24, 27
RAW = 4
LATE = 2 * COLS + (RAW + 2) * EDGE


def first_half(shape):
    return lax.broadcasted_iota(jnp.int32, shape, 1) < ROWS


def halves(x, y):
    return jnp.where(first_half(x.shape), x, y)


def doubled(x):
    other = pltpu.roll(x, ROWS, 1)
    return halves(x, other), halves(other, x)


def shift_cols(x, by):
    return pltpu.roll(x, (-by) % x.shape[0], 0)


def shift_rows(x, by):
    return pltpu.roll(x, (-by) % LANES, 1)


def in_plane(c, kx, ky, v):
    s = kx * (shift_cols(c, 1) - c) - v * c
    f = ky * (shift_rows(c, 1) - c)
    return (s - shift_cols(s, -1)) + (f - shift_rows(f, -1))


def face_x(k):
    return 0.5 * (k + shift_cols(k, 1))


def face_y(k):
    row = lax.rem(lax.broadcasted_iota(jnp.int32, k.shape, 1), ROWS)
    return jnp.where(row < ROWS - 1, 0.5 * (k + shift_rows(k, 1)), 0.0)


def couple(m_ref, kind, other):
    total = None
    for a in (-1, 0, 1):
        at_a = shift_rows(other, a) if a else other
        for b in (-1, 0, 1):
            term = m_ref[kind, 3 * (a + 1) + b + 1] * (shift_cols(at_a, b) if b else at_a)
            total = term if total is None else total + term
    return total


def slab_flags():
    slab = lax.axis_index("slab")
    upper = (slab > 0).astype(jnp.float32)
    lower = (slab < lax.axis_size("slab") - 1).astype(jnp.float32)
    return slab % 2 == 0, upper, lower


def faces_down(parity):
    return lax.axis_index("slab") % 2 == parity


def layer(down, i):
    return jnp.where(down, DEPTH - 1 - i, i)


def stream_even():
    return lax.axis_index("stream") % 2 == 0


def turned(first, second):
    return jnp.concatenate([first, second], axis=0).T


def pack_kernel(
    conc_in, kappa_in, vel_in, kind_in, row_in, col_in, w_in,
    msg_a, msg_b, raw_a, raw_b, conc, kappa, vel, active, faces,
    conc_s, kappa_s, vel_s, kind_s, row_s, col_s, w_s, sems,
):
    moves = [(conc_in, conc_s), (kappa_in, kappa_s), (vel_in, vel_s), (kind_in, kind_s)]
    moves += [(row_in, row_s), (col_in, col_s), (w_in, w_s)]
    copies = [pltpu.make_async_copy(*move, sems.at[i]) for i, move in enumerate(moves)]
    for copy in copies:
        copy.start()
    even = stream_even()

    def put(group, plane):
        head, tail = plane[:EDGE], plane[COLS - EDGE :]
        msg_a[group] = jnp.where(even, tail, head)
        msg_b[group] = jnp.where(even, head, tail)

    copies[0].wait()
    for z in range(DEPTH):
        conc[z] = turned(conc_s[0, z], conc_s[1, z])
        put(G_CONC + z, conc[z])
    copies[1].wait()
    for z in range(DEPTH):
        kappa[z] = turned(kappa_s[0, z], kappa_s[1, z])
        put(G_KAPPA + z, kappa[z])
    for copy in copies[2:]:
        copy.wait()
    row = lax.broadcasted_iota(jnp.int32, (ROWS, COLS), 0)
    col = lax.broadcasted_iota(jnp.int32, (ROWS, COLS), 1) + lax.axis_index("stream") * COLS
    for k in range(2):
        offsets = (row_s[k] - row).astype(jnp.float32), (col_s[k] - col).astype(jnp.float32)
        for i, item in enumerate(offsets + (w_s[k],)):
            faces[2 * i + k] = turned(item, item)
    for z in range(DEPTH):
        on = kind_s[z].astype(jnp.float32)
        vel[z] = turned(vel_s[z], vel_s[z])
        active[z] = turned(on, on)
        put(G_VT + z, halves(vel[z], active[z]))
    for i in range(3):
        put(G_FACE + i, halves(faces[2 * i], faces[2 * i + 1]))
    for parity, raw in enumerate((raw_a, raw_b)):
        down = faces_down(parity)
        z0, z1 = layer(down, 0), layer(down, 1)
        raw[0], raw[1], raw[2] = conc[z0], kappa[z0], kappa[z1]
        raw[3] = halves(vel[z0], active[z0])


class Halo:
    def __init__(self, got_a, got_b):
        self.got = got_a, got_b
        self.even = stream_even()

    def sides(self, group):
        a, b = self.got[0][group], self.got[1][group]
        return jnp.where(self.even, b, a), jnp.where(self.even, a, b)

    def plane(self, ref, z, group):
        left, right = self.sides(group + z)
        return jnp.concatenate([left, ref[z], right], axis=0)

    def pair(self, refs, places, group):
        left, right = [doubled(x) for x in self.sides(group)]
        return [
            jnp.concatenate([left[i], refs[i][places[i]], right[i]], axis=0) for i in range(2)
        ]

    def motion(self, vel, active, z):
        return self.pair((vel, active), (z, z), G_VT + z)


def edge_kernel(parity, conc, kappa, vel, active, got_a, got_b, faces, msg, edge_u, *made):
    halo = Halo(got_a, got_b)
    if made:
        m_out, = made
        planes = [halo.pair((faces, faces), (2 * i, 2 * i + 1), G_FACE + i) for i in range(3)]
        rate = jnp.where(first_half((TALL, LANES)), RATES[0], RATES[1])
        weights = [rate * planes[2][k] for k in range(2)]
        landed = None
        for a in (-1, 0, 1):
            parts = [jnp.where(planes[0][k] == a, weights[k], 0.0) for k in range(2)]
            here = None
            for b in (-1, 0, 1):
                hits = [jnp.where(planes[1][k] == b, parts[k], 0.0) for k in range(2)]
                total = hits[0] + hits[1]
                m_out[3 * (a + 1) + b + 1] = total
                total = shift_cols(total, -b) if b else total
                here = total if here is None else here + total
            here = shift_rows(here, -a) if a else here
            landed = here if landed is None else landed + here
        m_out[9] = landed
        m_out[10] = weights[0] + weights[1]
    else:
        m_out = faces

    down = faces_down(parity)
    _, upper, lower = slab_flags()
    z0, z1, z2 = [layer(down, i) for i in range(3)]
    hold = m_out[jnp.where(down, 10, 9)] * jnp.where(down, lower, upper)
    (v0, a0), (v1, a1) = [halo.motion(vel, active, z) for z in (z0, z1)]
    k0, k1, k2 = [halo.plane(kappa, z, G_KAPPA) for z in (z0, z1, z2)]
    c0, c1, c2 = [halo.plane(conc, z, G_CONC) for z in (z0, z1, z2)]
    kx0, ky0 = face_x(k0), face_y(k0)
    k01, k12 = 0.5 * (k0 + k1), 0.5 * (k1 + k2)
    flow = k01 * (c1 - c0)
    u0 = c0 + a0 * (in_plane(c0, kx0, ky0, v0) + flow - hold * c0)
    u1 = c1 + a1 * (in_plane(c1, face_x(k1), face_y(k1), v1) + k12 * (c2 - c1) - flow)
    w0 = u0 + a0 * (in_plane(u0, kx0, ky0, v0) + k01 * (u1 - u0) - hold * u0)
    edge_u[0] = u0
    edge_u[1] = w0
    upper_half = lax.broadcasted_iota(jnp.int32, (EDGE, LANES), 0) < EDGE // 2
    for i, x in enumerate((u0, w0, c0, k0, k1, halves(v0, a0))):
        if i < 2:
            msg[pl.ds(i * COLS, COLS)] = x[EDGE : EDGE + COLS]
        msg[pl.ds(2 * COLS + i * EDGE, EDGE)] = jnp.where(upper_half, x[EDGE + COLS :], x[:EDGE])
    if msg.shape[0] > LATE:
        msg[pl.ds(LATE, EDGE)] = jnp.zeros((EDGE, LANES), jnp.float32)


def block_kernel(
    conc, kappa, vel, active, got_a, got_b, m_ref,
    u3, middle, coef, av, both_m,
    cells, kx, ky, kz, own, move, on,
):
    halo = Halo(got_a, got_b)
    _, upper, lower = slab_flags()
    for a in (-1, 0, 1):
        for b in (-1, 0, 1):
            i = 3 * (a + 1) + b + 1
            both_m[0, i] = m_ref[i]
            there = shift_cols(m_ref[8 - i], b) if b else m_ref[8 - i]
            both_m[1, i] = shift_rows(there, a) if a else there
    both_m[0, 9] = m_ref[10]
    both_m[1, 9] = m_ref[9]
    zeros = jnp.zeros((TALL, LANES), jnp.float32)
    own[0] = m_ref[9] * upper
    own[1] = m_ref[10] * lower
    above = None
    for z in range(DEPTH):
        k = halo.plane(kappa, z, G_KAPPA)
        kx[z] = face_x(k)
        ky[z] = face_y(k)
        if z:
            kz[z] = 0.5 * (above + k)
        above = k
        cells[0, z] = halo.plane(conc, z, G_CONC)
        move[z], on[z] = halo.motion(vel, active, z)

    for parity in range(2):
        down = faces_down(parity)
        z0, z1, z2 = [layer(down, i) for i in range(3)]
        f01, f12 = jnp.where(down, DEPTH - 1, 1), jnp.where(down, DEPTH - 2, 2)
        for i, z in enumerate((z0, z1, z2)):
            av[parity, i] = on[z]
        for i, z in enumerate((z0, z1)):
            av[parity, 3 + i] = move[z]
        c0 = cells[0, z0]
        k01 = kz[f01]
        items = [kx[z0], ky[z0], kx[z1], ky[z1], k01, kz[f12]]
        items.append(k01 + own[jnp.where(down, 1, 0)])
        items.append(couple(both_m, jnp.where(down, 1, 0), c0))
        items += [halo.plane(kappa, z0, G_KAPPA), c0]
        for i, item in enumerate(items):
            coef[parity, i] = item

    for step in range(3):
        now, later = step % 2, (step + 1) % 2
        for z in range(DEPTH):
            c = cells[now, z]
            r = in_plane(c, kx[z], ky[z], move[z])
            if z < DEPTH - 1:
                r += kz[z + 1] * (cells[now, z + 1] - c)
            else:
                r -= own[1] * c
            if z:
                r -= kz[z] * (c - cells[now, z - 1])
            else:
                r -= own[0] * c
            new = c + on[z] * r
            if step == 2:
                u3[z] = new[EDGE : EDGE + COLS]
            else:
                cells[later, z] = new
    for z in range(3, DEPTH - 3):
        back = u3[z].T
        middle[0, z - 3] = back[:ROWS]
        middle[1, z - 3] = back[ROWS:]


def join_kernel(
    parity, coef, av, edge_u, m_ref, u3, middle, raw, late, *rest
):
    if parity == 0:
        raw_b, out, moved, result, sems = rest
        moved[0], moved[1] = doubled(raw_b[3])
        motion = doubled(raw[3])
    else:
        moved, _, out, result, sems = rest
        motion = moved[0], moved[1]
    down = faces_down(parity)
    start = jnp.where(down, DEPTH - 3, 0)
    copies = []
    if parity == 0:
        copies.append(pltpu.make_async_copy(middle, out.at[:, pl.ds(3, DEPTH - 6)], sems.at[0]))
        copies[-1].start()

    def ghost(i, main):
        edges = late[pl.ds(2 * COLS + i * EDGE, EDGE)]
        return jnp.concatenate([edges, main, edges], axis=0)

    ghost_c = [ghost(2, raw[0]), ghost(0, late[pl.ds(0, COLS)]), ghost(1, late[pl.ds(COLS, COLS)])]
    kg, kgg = ghost(3, raw[1]), ghost(4, raw[2])
    pads = doubled(late[pl.ds(2 * COLS + 5 * EDGE, EDGE)])
    vg, ag = [jnp.concatenate([pad, x, pad], axis=0) for pad, x in zip(pads, motion)]
    a0, a1, a2, v0, v1 = [av[parity, i] for i in range(5)]
    kx0, ky0, kx1, ky1, k01, k12, hold, first_to_g, k0, first_c = [
        coef[parity, i] for i in range(10)
    ]
    k_face, kg2 = 0.5 * (kg + k0), 0.5 * (kg + kgg)
    own_c = [first_c, edge_u[0], edge_u[1]]
    to_own, to_ghost = jnp.where(down, 0, 1), jnp.where(down, 1, 0)

    g, e = ghost_c[0], own_c[0]
    flow = k_face * (g - e)
    e1 = a0 * (flow + couple(m_ref, to_own, g))
    d1 = ag * (first_to_g - flow)
    g, e = ghost_c[1] + d1, own_c[1] + e1
    flow = k_face * (g - e)
    d2 = d1 + ag * (
        in_plane(d1, face_x(kg), face_y(kg), vg)
        - (kg2 + m_ref[to_ghost, 9]) * d1
        + (couple(m_ref, to_ghost, e) - flow)
    )
    e2 = e1 + a0 * (in_plane(e1, kx0, ky0, v0) - hold * e1 + (flow + couple(m_ref, to_own, g)))
    n2 = a1 * (k01 * e1)
    g, e = ghost_c[2] + d2, own_c[2] + e2
    flow = k_face * (g - e)
    e3 = e2 + a0 * (
        in_plane(e2, kx0, ky0, v0) - hold * e2 + k01 * n2 + (flow + couple(m_ref, to_own, g))
    )
    n3 = n2 + a1 * (in_plane(n2, kx1, ky1, v1) - (k01 + k12) * n2 + k01 * e2)
    m3 = a2 * (k12 * n2)
    for i, x in enumerate((e3, n3, m3)):
        z = layer(down, i)
        back = (u3[z] + x[EDGE : EDGE + COLS]).T
        result[0, z - start] = back[:ROWS]
        result[1, z - start] = back[ROWS:]
    copies.append(pltpu.make_async_copy(result, out.at[:, pl.ds(start, 3)], sems.at[1]))
    copies[-1].start()
    for copy in copies:
        copy.wait()


def swap(value, axis, parity):
    count = lax.axis_size(axis)
    pairs = []
    for i in range(parity, count - 1, 2):
        pairs += [(i, i + 1), (i + 1, i)]
    return lax.ppermute(value, axis, pairs)


def shape(*dims):
    return jax.ShapeDtypeStruct(dims, jnp.float32)


def call(kernel, outs, scratch=(), **specs):
    return pl.pallas_call(
        kernel,
        out_shape=outs,
        scratch_shapes=list(scratch),
        cost_estimate=pl.CostEstimate(flops=1024, bytes_accessed=1024, transcendentals=0),
        compiler_params=pltpu.CompilerParams(vmem_limit_bytes=40 * 2**20),
        **specs,
    )


def per_device(conc, kappa, velocity, cell_type, target_row, target_col, mortar_weight):
    tile = (ROWS, COLS)
    plane = (COLS, LANES)
    tall = (TALL, LANES)
    given = (conc, kappa, velocity, cell_type, target_row, target_col, mortar_weight)
    anywhere = pl.BlockSpec(memory_space=pl.ANY)
    whole = pl.BlockSpec(memory_space=pltpu.VMEM)

    msg_a, msg_b, raw_a, raw_b, *fields, faces = call(
        pack_kernel,
        [shape(GROUPS, EDGE, LANES)] * 2
        + [shape(RAW, *plane)] * 2
        + [shape(DEPTH, *plane)] * 4
        + [shape(6, *plane)],
        [pltpu.VMEM(x.shape, x.dtype) for x in given] + [pltpu.SemaphoreType.DMA((7,))],
        in_specs=[anywhere] * 7,
    )(*[pltpu.with_memory_space_constraint(x, pltpu.HBM) for x in given])
    got_b = swap(msg_b, "stream", 1)
    got_a = swap(msg_a, "stream", 0)
    raw_b = swap(raw_b, "slab", 1)
    raw_a = swap(raw_a, "slab", 0)
    fields += [got_a, got_b]
    late_b, edge_b, m = call(
        functools.partial(edge_kernel, 1),
        (shape(LATE + EDGE, LANES), shape(2, *tall), shape(11, *tall)),
    )(*fields, faces)
    late_b = swap(late_b, "slab", 1)
    late_a, edge_a = call(
        functools.partial(edge_kernel, 0), (shape(LATE, LANES), shape(2, *tall))
    )(*fields, m)
    late_a = swap(late_a, "slab", 0)
    u3, middle, coef, av, both_m = call(
        block_kernel,
        (
            shape(DEPTH, *plane),
            shape(2, DEPTH - 6, *tile),
            shape(2, 10, *tall),
            shape(2, 5, *tall),
            shape(2, 10, *tall),
        ),
        (
            pltpu.VMEM((2, DEPTH) + tall, jnp.float32),
            pltpu.VMEM((DEPTH,) + tall, jnp.float32),
            pltpu.VMEM((DEPTH,) + tall, jnp.float32),
            pltpu.VMEM((DEPTH,) + tall, jnp.float32),
            pltpu.VMEM((2,) + tall, jnp.float32),
            pltpu.VMEM((DEPTH,) + tall, jnp.float32),
            pltpu.VMEM((DEPTH,) + tall, jnp.float32),
        ),
    )(*fields, m)

    def join(parity, outs, out_specs, edge_u, raw, late, *more, aliases={}):
        return call(
            functools.partial(join_kernel, parity),
            outs,
            (pltpu.VMEM((2, 3) + tile, jnp.float32), pltpu.SemaphoreType.DMA((2,))),
            in_specs=[whole] * 9 + [anywhere] * (len(more) - 1),
            out_specs=out_specs,
            input_output_aliases=aliases,
        )(coef, av, edge_u, both_m, u3, middle, raw, late, *more)

    final = shape(2, DEPTH, *tile)
    out, moved = join(
        0, (final, shape(2, *plane)), (anywhere, whole), edge_a, raw_a, late_a, raw_b
    )
    return join(1, final, anywhere, edge_b, raw_b, late_b, moved, out, aliases={9: 0})


def solution(mesh):
    return jax.shard_map(
        per_device,
        mesh=mesh,
        in_specs=(
            P(None, "slab", None, "stream"),
            P(None, "slab", None, "stream"),
            P("slab", None, "stream"),
            P("slab", None, "stream"),
            P(None, None, "stream"),
            P(None, None, "stream"),
            P(None, None, "stream"),
        ),
        out_specs=P(None, "slab", None, "stream"),
        check_vma=False,
    )
```

```python
import functools

import jax
import jax.numpy as jnp
from jax import lax
from jax.experimental import pallas as pl
from jax.experimental.pallas import tpu as pltpu
from jax.sharding import PartitionSpec as P

RATES = (0.08, 0.12)
DEPTH, ROWS, COLS = 8, 64, 128
LANES = 2 * ROWS
EDGE = 8
TALL = COLS + 2 * EDGE
G_CONC, G_KAPPA, G_VT, G_FACE, GROUPS = 0, 8, 16, 24, 27
RAW = 4
LATE = 2 * COLS + (RAW + 2) * EDGE


def first_half(shape):
    return lax.broadcasted_iota(jnp.int32, shape, 1) < ROWS


def halves(x, y):
    return jnp.where(first_half(x.shape), x, y)


def doubled(x):
    other = pltpu.roll(x, ROWS, 1)
    return halves(x, other), halves(other, x)


def shift_cols(x, by):
    return pltpu.roll(x, (-by) % x.shape[0], 0)


def shift_rows(x, by):
    return pltpu.roll(x, (-by) % LANES, 1)


def in_plane(c, kx, ky, v):
    s = kx * (shift_cols(c, 1) - c) - v * c
    f = ky * (shift_rows(c, 1) - c)
    return (s - shift_cols(s, -1)) + (f - shift_rows(f, -1))


def face_x(k):
    return 0.5 * (k + shift_cols(k, 1))


def face_y(k):
    row = lax.rem(lax.broadcasted_iota(jnp.int32, k.shape, 1), ROWS)
    return jnp.where(row < ROWS - 1, 0.5 * (k + shift_rows(k, 1)), 0.0)


def couple(m_ref, kind, other):
    rows = [shift_rows(other, -1), other, shift_rows(other, 1)]
    total = None
    for b in (-1, 0, 1):
        part = None
        for a in (-1, 0, 1):
            term = m_ref[kind, 3 * (a + 1) + b + 1] * rows[a + 1]
            part = term if part is None else part + term
        part = shift_cols(part, b) if b else part
        total = part if total is None else total + part
    return total


def slab_flags():
    slab = lax.axis_index("slab")
    upper = (slab > 0).astype(jnp.float32)
    lower = (slab < lax.axis_size("slab") - 1).astype(jnp.float32)
    return slab % 2 == 0, upper, lower


def faces_down(parity):
    return lax.axis_index("slab") % 2 == parity


def layer(down, i):
    return jnp.where(down, DEPTH - 1 - i, i)


def stream_even():
    return lax.axis_index("stream") % 2 == 0


def turned(first, second):
    return jnp.concatenate([first, second], axis=0).T


def pack_kernel(
    conc_in, kappa_in, vel_in, kind_in, row_in, col_in, w_in,
    msg_a, msg_b, raw_a, raw_b, conc, kappa, mixed, faces,
    conc_s, kappa_s, vel_s, kind_s, row_s, col_s, w_s, sems,
):
    moves = [(conc_in, conc_s), (kappa_in, kappa_s), (vel_in, vel_s), (kind_in, kind_s)]
    moves += [(row_in, row_s), (col_in, col_s), (w_in, w_s)]
    copies = [pltpu.make_async_copy(*move, sems.at[i]) for i, move in enumerate(moves)]
    for copy in copies:
        copy.start()
    even = stream_even()

    def put(group, plane):
        head, tail = plane[:EDGE], plane[COLS - EDGE :]
        msg_a[group] = jnp.where(even, tail, head)
        msg_b[group] = jnp.where(even, head, tail)

    copies[0].wait()
    for z in range(DEPTH):
        conc[z] = turned(conc_s[0, z], conc_s[1, z])
        put(G_CONC + z, conc[z])
    copies[1].wait()
    for z in range(DEPTH):
        kappa[z] = turned(kappa_s[0, z], kappa_s[1, z])
        put(G_KAPPA + z, kappa[z])
    for copy in copies[2:]:
        copy.wait()
    row = lax.broadcasted_iota(jnp.int32, (ROWS, COLS), 0)
    col = lax.broadcasted_iota(jnp.int32, (ROWS, COLS), 1) + lax.axis_index("stream") * COLS
    for k in range(2):
        offsets = (row_s[k] - row).astype(jnp.float32), (col_s[k] - col).astype(jnp.float32)
        for i, item in enumerate(offsets + (w_s[k],)):
            faces[2 * i + k] = turned(item, item)
    for z in range(DEPTH):
        mixed[z] = turned(vel_s[z], kind_s[z].astype(jnp.float32))
        put(G_VT + z, mixed[z])
    for i in range(3):
        put(G_FACE + i, halves(faces[2 * i], faces[2 * i + 1]))
    for parity, raw in enumerate((raw_a, raw_b)):
        down = faces_down(parity)
        z0, z1 = layer(down, 0), layer(down, 1)
        raw[0], raw[1], raw[2], raw[3] = conc[z0], kappa[z0], kappa[z1], mixed[z0]


class Halo:
    def __init__(self, got_a, got_b):
        self.got = got_a, got_b
        self.even = stream_even()

    def sides(self, group):
        a, b = self.got[0][group], self.got[1][group]
        return jnp.where(self.even, b, a), jnp.where(self.even, a, b)

    def plane(self, ref, z, group):
        left, right = self.sides(group + z)
        return jnp.concatenate([left, ref[z], right], axis=0)

    def pair(self, refs, places, group):
        left, right = [doubled(x) for x in self.sides(group)]
        return [
            jnp.concatenate([left[i], refs[i][places[i]], right[i]], axis=0) for i in range(2)
        ]

    def motion(self, mixed, z):
        return doubled(self.plane(mixed, z, G_VT))


def edge_kernel(parity, conc, kappa, mixed, got_a, got_b, faces, msg, edge_u, *made):
    halo = Halo(got_a, got_b)
    if made:
        m_out, = made
        planes = [halo.pair((faces, faces), (2 * i, 2 * i + 1), G_FACE + i) for i in range(3)]
        rate = jnp.where(first_half((TALL, LANES)), RATES[0], RATES[1])
        weights = [rate * planes[2][k] for k in range(2)]
        landed = None
        for a in (-1, 0, 1):
            parts = [jnp.where(planes[0][k] == a, weights[k], 0.0) for k in range(2)]
            here = None
            for b in (-1, 0, 1):
                hits = [jnp.where(planes[1][k] == b, parts[k], 0.0) for k in range(2)]
                total = hits[0] + hits[1]
                m_out[3 * (a + 1) + b + 1] = total
                total = shift_cols(total, -b) if b else total
                here = total if here is None else here + total
            here = shift_rows(here, -a) if a else here
            landed = here if landed is None else landed + here
        m_out[9] = landed
        m_out[10] = weights[0] + weights[1]
    else:
        m_out = faces

    down = faces_down(parity)
    _, upper, lower = slab_flags()
    z0, z1, z2 = [layer(down, i) for i in range(3)]
    hold = m_out[jnp.where(down, 10, 9)] * jnp.where(down, lower, upper)
    (v0, a0), (v1, a1) = [halo.motion(mixed, z) for z in (z0, z1)]
    k0, k1, k2 = [halo.plane(kappa, z, G_KAPPA) for z in (z0, z1, z2)]
    c0, c1, c2 = [halo.plane(conc, z, G_CONC) for z in (z0, z1, z2)]
    kx0, ky0 = face_x(k0), face_y(k0)
    k01, k12 = 0.5 * (k0 + k1), 0.5 * (k1 + k2)
    flow = k01 * (c1 - c0)
    u0 = c0 + a0 * (in_plane(c0, kx0, ky0, v0) + flow - hold * c0)
    u1 = c1 + a1 * (in_plane(c1, face_x(k1), face_y(k1), v1) + k12 * (c2 - c1) - flow)
    w0 = u0 + a0 * (in_plane(u0, kx0, ky0, v0) + k01 * (u1 - u0) - hold * u0)
    edge_u[0] = u0
    edge_u[1] = w0
    upper_half = lax.broadcasted_iota(jnp.int32, (EDGE, LANES), 0) < EDGE // 2
    for i, x in enumerate((u0, w0, c0, k0, k1, halves(v0, a0))):
        if i < 2:
            msg[pl.ds(i * COLS, COLS)] = x[EDGE : EDGE + COLS]
        msg[pl.ds(2 * COLS + i * EDGE, EDGE)] = jnp.where(upper_half, x[EDGE + COLS :], x[:EDGE])
    if msg.shape[0] > LATE:
        msg[pl.ds(LATE, EDGE)] = jnp.zeros((EDGE, LANES), jnp.float32)


def block_kernel(
    conc, kappa, mixed, got_a, got_b, m_ref,
    u3, middle, coef, av, both_m,
    cells, kx, ky, kz, own, move, on,
):
    halo = Halo(got_a, got_b)
    _, upper, lower = slab_flags()
    for a in (-1, 0, 1):
        for b in (-1, 0, 1):
            i = 3 * (a + 1) + b + 1
            both_m[0, i] = shift_cols(m_ref[i], -b) if b else m_ref[i]
            both_m[1, i] = shift_rows(m_ref[8 - i], a) if a else m_ref[8 - i]
    both_m[0, 9] = m_ref[10]
    both_m[1, 9] = m_ref[9]
    zeros = jnp.zeros((TALL, LANES), jnp.float32)
    own[0] = m_ref[9] * upper
    own[1] = m_ref[10] * lower
    above = None
    for z in range(DEPTH):
        k = halo.plane(kappa, z, G_KAPPA)
        kx[z] = face_x(k)
        ky[z] = face_y(k)
        if z:
            kz[z] = 0.5 * (above + k)
        above = k
        cells[0, z] = halo.plane(conc, z, G_CONC)
        move[z], on[z] = halo.motion(mixed, z)

    for parity in range(2):
        down = faces_down(parity)
        z0, z1, z2 = [layer(down, i) for i in range(3)]
        f01, f12 = jnp.where(down, DEPTH - 1, 1), jnp.where(down, DEPTH - 2, 2)
        for i, z in enumerate((z0, z1, z2)):
            av[parity, i] = on[z]
        for i, z in enumerate((z0, z1)):
            av[parity, 3 + i] = move[z]
        c0 = cells[0, z0]
        k01 = kz[f01]
        items = [kx[z0], ky[z0], kx[z1], ky[z1], k01, kz[f12]]
        items.append(k01 + own[jnp.where(down, 1, 0)])
        items.append(couple(both_m, jnp.where(down, 1, 0), c0))
        items += [halo.plane(kappa, z0, G_KAPPA), c0]
        for i, item in enumerate(items):
            coef[parity, i] = item

    for step in range(3):
        now, later = step % 2, (step + 1) % 2
        for z in range(DEPTH):
            c = cells[now, z]
            r = in_plane(c, kx[z], ky[z], move[z])
            if z < DEPTH - 1:
                r += kz[z + 1] * (cells[now, z + 1] - c)
            else:
                r -= own[1] * c
            if z:
                r -= kz[z] * (c - cells[now, z - 1])
            else:
                r -= own[0] * c
            new = c + on[z] * r
            if step == 2:
                u3[z] = new[EDGE : EDGE + COLS]
            else:
                cells[later, z] = new
    for z in range(3, DEPTH - 3):
        back = u3[z].T
        middle[0, z - 3] = back[:ROWS]
        middle[1, z - 3] = back[ROWS:]


def join_kernel(
    parity, coef, av, edge_u, m_ref, u3, raw, late, *rest
):
    down = faces_down(parity)
    copies = []

    def send(source, target):
        copies.append(pltpu.make_async_copy(source, target, sems.at[len(copies)]))
        copies[-1].start()

    if parity == 0:
        _, result = rest
    else:
        joined, middle, out, result, sems = rest
        send(middle, out.at[:, pl.ds(3, DEPTH - 6)])
        for i in range(3):
            send(joined.at[:, i], out.at[:, layer(faces_down(0), i)])

    def ghost(i, main):
        edges = late[pl.ds(2 * COLS + i * EDGE, EDGE)]
        return jnp.concatenate([edges, main, edges], axis=0)

    ghost_c = [ghost(2, raw[0]), ghost(0, late[pl.ds(0, COLS)]), ghost(1, late[pl.ds(COLS, COLS)])]
    kg, kgg = ghost(3, raw[1]), ghost(4, raw[2])
    vg, ag = doubled(ghost(5, raw[3]))
    a0, a1, a2, v0, v1 = [av[parity, i] for i in range(5)]
    kx0, ky0, kx1, ky1, k01, k12, hold, first_to_g, k0, first_c = [
        coef[parity, i] for i in range(10)
    ]
    k_face, kg2 = 0.5 * (kg + k0), 0.5 * (kg + kgg)
    own_c = [first_c, edge_u[0], edge_u[1]]
    to_own, to_ghost = jnp.where(down, 0, 1), jnp.where(down, 1, 0)

    g, e = ghost_c[0], own_c[0]
    flow = k_face * (g - e)
    e1 = a0 * (flow + couple(m_ref, to_own, g))
    d1 = ag * (first_to_g - flow)
    g, e = ghost_c[1] + d1, own_c[1] + e1
    flow = k_face * (g - e)
    d2 = d1 + ag * (
        in_plane(d1, face_x(kg), face_y(kg), vg)
        - (kg2 + m_ref[to_ghost, 9]) * d1
        + (couple(m_ref, to_ghost, e) - flow)
    )
    e2 = e1 + a0 * (in_plane(e1, kx0, ky0, v0) - hold * e1 + (flow + couple(m_ref, to_own, g)))
    n2 = a1 * (k01 * e1)

    def finish(i, x):
        z = layer(down, i)
        back = (u3[z] + x[EDGE : EDGE + COLS]).T
        result[0, i] = back[:ROWS]
        result[1, i] = back[ROWS:]
        if parity:
            send(result.at[:, i], out.at[:, z])

    finish(2, a2 * (k12 * n2))
    finish(1, n2 + a1 * (in_plane(n2, kx1, ky1, v1) - (k01 + k12) * n2 + k01 * e2))
    g, e = ghost_c[2] + d2, own_c[2] + e2
    flow = k_face * (g - e)
    finish(
        0,
        e2
        + a0
        * (
            in_plane(e2, kx0, ky0, v0) - hold * e2 + k01 * n2
            + (flow + couple(m_ref, to_own, g))
        ),
    )
    for copy in copies:
        copy.wait()


def swap(value, axis, parity):
    count = lax.axis_size(axis)
    pairs = []
    for i in range(parity, count - 1, 2):
        pairs += [(i, i + 1), (i + 1, i)]
    return lax.ppermute(value, axis, pairs)


def shape(*dims):
    return jax.ShapeDtypeStruct(dims, jnp.float32)


def call(kernel, outs, scratch=(), **specs):
    return pl.pallas_call(
        kernel,
        out_shape=outs,
        scratch_shapes=list(scratch),
        cost_estimate=pl.CostEstimate(flops=1024, bytes_accessed=1024, transcendentals=0),
        compiler_params=pltpu.CompilerParams(vmem_limit_bytes=40 * 2**20),
        **specs,
    )


def per_device(conc, kappa, velocity, cell_type, target_row, target_col, mortar_weight):
    tile = (ROWS, COLS)
    plane = (COLS, LANES)
    tall = (TALL, LANES)
    given = (conc, kappa, velocity, cell_type, target_row, target_col, mortar_weight)
    anywhere = pl.BlockSpec(memory_space=pl.ANY)
    whole = pl.BlockSpec(memory_space=pltpu.VMEM)

    msg_a, msg_b, raw_a, raw_b, *fields, faces = call(
        pack_kernel,
        [shape(GROUPS, EDGE, LANES)] * 2
        + [shape(RAW, *plane)] * 2
        + [shape(DEPTH, *plane)] * 3
        + [shape(6, *plane)],
        [pltpu.VMEM(x.shape, x.dtype) for x in given] + [pltpu.SemaphoreType.DMA((7,))],
        in_specs=[anywhere] * 7,
    )(*[pltpu.with_memory_space_constraint(x, pltpu.HBM) for x in given])
    got_b = swap(msg_b, "stream", 1)
    got_a = swap(msg_a, "stream", 0)
    raw_b = swap(raw_b, "slab", 1)
    raw_a = swap(raw_a, "slab", 0)
    fields += [got_a, got_b]
    late_b, edge_b, m = call(
        functools.partial(edge_kernel, 1),
        (shape(LATE + EDGE, LANES), shape(2, *tall), shape(11, *tall)),
    )(*fields, faces)
    late_b = swap(late_b, "slab", 1)
    late_a, edge_a = call(
        functools.partial(edge_kernel, 0), (shape(LATE, LANES), shape(2, *tall))
    )(*fields, m)
    late_a = swap(late_a, "slab", 0)
    u3, middle, coef, av, both_m = call(
        block_kernel,
        (
            shape(DEPTH, *plane),
            shape(2, DEPTH - 6, *tile),
            shape(2, 10, *tall),
            shape(2, 5, *tall),
            shape(2, 10, *tall),
        ),
        (
            pltpu.VMEM((2, DEPTH) + tall, jnp.float32),
            pltpu.VMEM((DEPTH,) + tall, jnp.float32),
            pltpu.VMEM((DEPTH,) + tall, jnp.float32),
            pltpu.VMEM((DEPTH,) + tall, jnp.float32),
            pltpu.VMEM((2,) + tall, jnp.float32),
            pltpu.VMEM((DEPTH,) + tall, jnp.float32),
            pltpu.VMEM((DEPTH,) + tall, jnp.float32),
        ),
    )(*fields, m)

    def join(parity, operands, extra, outs, **specs):
        return call(
            functools.partial(join_kernel, parity),
            outs,
            in_specs=[whole] * (4 + len(operands)) + [anywhere] * len(extra),
            **specs,
        )(coef, av, operands[0], both_m, u3, *operands[1:], *extra)

    joined = join(0, (edge_a, raw_a, late_a), (raw_b,), shape(2, 3, *tile))
    return join(
        1,
        (edge_b, raw_b, late_b, joined, middle),
        (),
        shape(2, DEPTH, *tile),
        scratch=(pltpu.VMEM((2, 3) + tile, jnp.float32), pltpu.SemaphoreType.DMA((7,))),
        out_specs=anywhere,
    )


def solution(mesh):
    return jax.shard_map(
        per_device,
        mesh=mesh,
        in_specs=(
            P(None, "slab", None, "stream"),
            P(None, "slab", None, "stream"),
            P("slab", None, "stream"),
            P("slab", None, "stream"),
            P(None, None, "stream"),
            P(None, None, "stream"),
            P(None, None, "stream"),
        ),
        out_specs=P(None, "slab", None, "stream"),
        check_vma=False,
    )
```

```python
import functools

import jax
import jax.numpy as jnp
from jax import lax
from jax.experimental import pallas as pl
from jax.experimental.pallas import tpu as pltpu
from jax.sharding import PartitionSpec as P

RATES = (0.08, 0.12)
DEPTH, ROWS, COLS = 8, 64, 128
LANES = 2 * ROWS
EDGE = 8
TALL = COLS + 2 * EDGE
G_CONC, G_KAPPA, G_VT, G_FACE, GROUPS = 0, 8, 16, 24, 27
RAW = 4
LATE = 2 * COLS + (RAW + 1) * EDGE


def first_half(shape):
    return lax.broadcasted_iota(jnp.int32, shape, 1) < ROWS


def halves(x, y):
    return jnp.where(first_half(x.shape), x, y)


def doubled(x):
    other = pltpu.roll(x, ROWS, 1)
    return halves(x, other), halves(other, x)


def shift_cols(x, by):
    return pltpu.roll(x, (-by) % x.shape[0], 0)


def shift_rows(x, by):
    return pltpu.roll(x, (-by) % LANES, 1)


def in_plane(c, kx, ky, v):
    s = kx * (shift_cols(c, 1) - c) - v * c
    f = ky * (shift_rows(c, 1) - c)
    return (s - shift_cols(s, -1)) + (f - shift_rows(f, -1))


def face_x(k):
    return 0.5 * (k + shift_cols(k, 1))


def face_y(k):
    row = lax.rem(lax.broadcasted_iota(jnp.int32, k.shape, 1), ROWS)
    return jnp.where(row < ROWS - 1, 0.5 * (k + shift_rows(k, 1)), 0.0)


def couple(m_ref, kind, other):
    rows = [shift_rows(other, -1), other, shift_rows(other, 1)]
    total = None
    for b in (-1, 0, 1):
        part = None
        for a in (-1, 0, 1):
            term = m_ref[kind, 3 * (a + 1) + b + 1] * rows[a + 1]
            part = term if part is None else part + term
        part = shift_cols(part, b) if b else part
        total = part if total is None else total + part
    return total


def slab_flags():
    slab = lax.axis_index("slab")
    upper = (slab > 0).astype(jnp.float32)
    lower = (slab < lax.axis_size("slab") - 1).astype(jnp.float32)
    return slab % 2 == 0, upper, lower


def faces_down(parity):
    return lax.axis_index("slab") % 2 == parity


def layer(down, i):
    return jnp.where(down, DEPTH - 1 - i, i)


def stream_even():
    return lax.axis_index("stream") % 2 == 0


def turned(first, second):
    return jnp.concatenate([first, second], axis=0).T


def pack_kernel(
    conc_in, kappa_in, vel_in, kind_in, row_in, col_in, w_in,
    msg_a, msg_b, raw_a, raw_b, conc, kappa, mixed, faces,
    conc_s, kappa_s, vel_s, kind_s, row_s, col_s, w_s, sems,
):
    moves = [(conc_in, conc_s), (kappa_in, kappa_s), (vel_in, vel_s), (kind_in, kind_s)]
    moves += [(row_in, row_s), (col_in, col_s), (w_in, w_s)]
    copies = [pltpu.make_async_copy(*move, sems.at[i]) for i, move in enumerate(moves)]
    for copy in copies:
        copy.start()
    even = stream_even()

    def put(group, plane):
        head, tail = plane[:EDGE], plane[COLS - EDGE :]
        msg_a[group] = jnp.where(even, tail, head)
        msg_b[group] = jnp.where(even, head, tail)

    copies[0].wait()
    for z in range(DEPTH):
        conc[z] = turned(conc_s[0, z], conc_s[1, z])
        put(G_CONC + z, conc[z])
    copies[1].wait()
    for z in range(DEPTH):
        kappa[z] = turned(kappa_s[0, z], kappa_s[1, z])
        put(G_KAPPA + z, kappa[z])
    for copy in copies[2:]:
        copy.wait()
    row = lax.broadcasted_iota(jnp.int32, (ROWS, COLS), 0)
    col = lax.broadcasted_iota(jnp.int32, (ROWS, COLS), 1) + lax.axis_index("stream") * COLS
    for k in range(2):
        offsets = (row_s[k] - row).astype(jnp.float32), (col_s[k] - col).astype(jnp.float32)
        for i, item in enumerate(offsets + (w_s[k],)):
            faces[2 * i + k] = turned(item, item)
    for z in range(DEPTH):
        mixed[z] = turned(vel_s[z], kind_s[z].astype(jnp.float32))
        put(G_VT + z, mixed[z])
    for i in range(3):
        put(G_FACE + i, halves(faces[2 * i], faces[2 * i + 1]))
    for parity, raw in enumerate((raw_a, raw_b)):
        down = faces_down(parity)
        z0, z1 = layer(down, 0), layer(down, 1)
        raw[0], raw[1], raw[2], raw[3] = conc[z0], kappa[z0], kappa[z1], mixed[z0]


class Halo:
    def __init__(self, got_a, got_b):
        self.got = got_a, got_b
        self.even = stream_even()

    def sides(self, group):
        a, b = self.got[0][group], self.got[1][group]
        return jnp.where(self.even, b, a), jnp.where(self.even, a, b)

    def plane(self, ref, z, group):
        left, right = self.sides(group + z)
        return jnp.concatenate([left, ref[z], right], axis=0)

    def pair(self, refs, places, group):
        left, right = [doubled(x) for x in self.sides(group)]
        return [
            jnp.concatenate([left[i], refs[i][places[i]], right[i]], axis=0) for i in range(2)
        ]

    def motion(self, mixed, z):
        return doubled(self.plane(mixed, z, G_VT))


def edge_kernel(parity, conc, kappa, mixed, got_a, got_b, faces, msg, edge_u, *made):
    halo = Halo(got_a, got_b)
    if made:
        m_out, = made
        planes = [halo.pair((faces, faces), (2 * i, 2 * i + 1), G_FACE + i) for i in range(3)]
        rate = jnp.where(first_half((TALL, LANES)), RATES[0], RATES[1])
        weights = [rate * planes[2][k] for k in range(2)]
        landed = None
        for a in (-1, 0, 1):
            parts = [jnp.where(planes[0][k] == a, weights[k], 0.0) for k in range(2)]
            here = None
            for b in (-1, 0, 1):
                hits = [jnp.where(planes[1][k] == b, parts[k], 0.0) for k in range(2)]
                total = hits[0] + hits[1]
                m_out[3 * (a + 1) + b + 1] = total
                total = shift_cols(total, -b) if b else total
                here = total if here is None else here + total
            here = shift_rows(here, -a) if a else here
            landed = here if landed is None else landed + here
        m_out[9] = landed
        m_out[10] = weights[0] + weights[1]
    else:
        m_out = faces

    down = faces_down(parity)
    _, upper, lower = slab_flags()
    z0, z1, z2 = [layer(down, i) for i in range(3)]
    hold = m_out[jnp.where(down, 10, 9)] * jnp.where(down, lower, upper)
    (v0, a0), (v1, a1) = [halo.motion(mixed, z) for z in (z0, z1)]
    k0, k1, k2 = [halo.plane(kappa, z, G_KAPPA) for z in (z0, z1, z2)]
    c0, c1, c2 = [halo.plane(conc, z, G_CONC) for z in (z0, z1, z2)]
    kx0, ky0 = face_x(k0), face_y(k0)
    k01, k12 = 0.5 * (k0 + k1), 0.5 * (k1 + k2)
    flow = k01 * (c1 - c0)
    u0 = c0 + a0 * (in_plane(c0, kx0, ky0, v0) + flow - hold * c0)
    u1 = c1 + a1 * (in_plane(c1, face_x(k1), face_y(k1), v1) + k12 * (c2 - c1) - flow)
    w0 = u0 + a0 * (in_plane(u0, kx0, ky0, v0) + k01 * (u1 - u0) - hold * u0)
    edge_u[0] = u0
    edge_u[1] = w0
    upper_half = lax.broadcasted_iota(jnp.int32, (EDGE, LANES), 0) < EDGE // 2
    for i, x in enumerate((u0, w0, c0, k0, k1, halves(v0, a0))):
        if i < 2:
            msg[pl.ds(i * COLS, COLS)] = x[EDGE : EDGE + COLS]
        edges = jnp.where(upper_half, x[EDGE + COLS :], x[:EDGE])
        if i == 0:
            outer = edges
        elif i == 1:
            at = lax.broadcasted_iota(jnp.int32, (EDGE, LANES), 0)
            inner = jnp.where(upper_half, pltpu.roll(edges, 2, 0), pltpu.roll(edges, EDGE - 2, 0))
            msg[pl.ds(2 * COLS, EDGE)] = jnp.where((at < 2) | (at >= EDGE - 2), outer, inner)
        else:
            msg[pl.ds(2 * COLS + (i - 1) * EDGE, EDGE)] = edges
    if msg.shape[0] > LATE:
        msg[pl.ds(LATE, EDGE)] = jnp.zeros((EDGE, LANES), jnp.float32)


def block_kernel(
    conc, kappa, mixed, got_a, got_b, m_ref,
    u3, middle, coef, av, both_m,
    cells, kx, ky, kz, own, move, on,
):
    halo = Halo(got_a, got_b)
    _, upper, lower = slab_flags()
    for a in (-1, 0, 1):
        for b in (-1, 0, 1):
            i = 3 * (a + 1) + b + 1
            both_m[0, i] = shift_cols(m_ref[i], -b) if b else m_ref[i]
            both_m[1, i] = shift_rows(m_ref[8 - i], a) if a else m_ref[8 - i]
    both_m[0, 9] = m_ref[10]
    both_m[1, 9] = m_ref[9]
    zeros = jnp.zeros((TALL, LANES), jnp.float32)
    own[0] = m_ref[9] * upper
    own[1] = m_ref[10] * lower
    above = None
    for z in range(DEPTH):
        k = halo.plane(kappa, z, G_KAPPA)
        kx[z] = face_x(k)
        ky[z] = face_y(k)
        if z:
            kz[z] = 0.5 * (above + k)
        above = k
        cells[0, z] = halo.plane(conc, z, G_CONC)
        move[z], on[z] = halo.motion(mixed, z)

    for parity in range(2):
        down = faces_down(parity)
        z0, z1, z2 = [layer(down, i) for i in range(3)]
        f01, f12 = jnp.where(down, DEPTH - 1, 1), jnp.where(down, DEPTH - 2, 2)
        for i, z in enumerate((z0, z1, z2)):
            av[parity, i] = on[z]
        for i, z in enumerate((z0, z1)):
            av[parity, 3 + i] = move[z]
        c0 = cells[0, z0]
        k01 = kz[f01]
        items = [kx[z0], ky[z0], kx[z1], ky[z1], k01, kz[f12]]
        items.append(k01 + own[jnp.where(down, 1, 0)])
        items.append(couple(both_m, jnp.where(down, 1, 0), c0))
        items += [halo.plane(kappa, z0, G_KAPPA), c0]
        for i, item in enumerate(items):
            coef[parity, i] = item

    for step in range(3):
        now, later = step % 2, (step + 1) % 2
        for z in range(DEPTH):
            c = cells[now, z]
            r = in_plane(c, kx[z], ky[z], move[z])
            if z < DEPTH - 1:
                r += kz[z + 1] * (cells[now, z + 1] - c)
            else:
                r -= own[1] * c
            if z:
                r -= kz[z] * (c - cells[now, z - 1])
            else:
                r -= own[0] * c
            new = c + on[z] * r
            if step == 2:
                u3[z] = new[EDGE : EDGE + COLS]
            else:
                cells[later, z] = new
    for z in range(3, DEPTH - 3):
        back = u3[z].T
        middle[0, z - 3] = back[:ROWS]
        middle[1, z - 3] = back[ROWS:]


def join_kernel(
    parity, coef, av, edge_u, m_ref, u3, raw, late, *rest
):
    down = faces_down(parity)
    copies = []

    def send(source, target):
        copies.append(pltpu.make_async_copy(source, target, sems.at[len(copies)]))
        copies[-1].start()

    if parity == 0:
        _, result = rest
    else:
        joined, middle, out, result, sems = rest
        send(middle, out.at[:, pl.ds(3, DEPTH - 6)])
        for i in range(3):
            send(joined.at[:, i], out.at[:, layer(faces_down(0), i)])

    def ghost(i, main):
        edges = late[pl.ds(2 * COLS + max(i - 1, 0) * EDGE, EDGE)]
        if i == 1:
            at = lax.broadcasted_iota(jnp.int32, (EDGE, LANES), 0)
            edges = jnp.where(at < EDGE // 2, pltpu.roll(edges, EDGE - 2, 0), pltpu.roll(edges, 2, 0))
        return jnp.concatenate([edges, main, edges], axis=0)

    ghost_c = [ghost(2, raw[0]), ghost(0, late[pl.ds(0, COLS)]), ghost(1, late[pl.ds(COLS, COLS)])]
    kg, kgg = ghost(3, raw[1]), ghost(4, raw[2])
    vg, ag = doubled(ghost(5, raw[3]))
    a0, a1, a2, v0, v1 = [av[parity, i] for i in range(5)]
    kx0, ky0, kx1, ky1, k01, k12, hold, first_to_g, k0, first_c = [
        coef[parity, i] for i in range(10)
    ]
    k_face, kg2 = 0.5 * (kg + k0), 0.5 * (kg + kgg)
    own_c = [first_c, edge_u[0], edge_u[1]]
    to_own, to_ghost = jnp.where(down, 0, 1), jnp.where(down, 1, 0)

    g, e = ghost_c[0], own_c[0]
    flow = k_face * (g - e)
    e1 = a0 * (flow + couple(m_ref, to_own, g))
    d1 = ag * (first_to_g - flow)
    g, e = ghost_c[1] + d1, own_c[1] + e1
    flow = k_face * (g - e)
    d2 = d1 + ag * (
        in_plane(d1, face_x(kg), face_y(kg), vg)
        - (kg2 + m_ref[to_ghost, 9]) * d1
        + (couple(m_ref, to_ghost, e) - flow)
    )
    e2 = e1 + a0 * (in_plane(e1, kx0, ky0, v0) - hold * e1 + (flow + couple(m_ref, to_own, g)))
    n2 = a1 * (k01 * e1)

    def finish(i, x):
        z = layer(down, i)
        back = (u3[z] + x[EDGE : EDGE + COLS]).T
        result[0, i] = back[:ROWS]
        result[1, i] = back[ROWS:]
        if parity:
            send(result.at[:, i], out.at[:, z])

    finish(2, a2 * (k12 * n2))
    finish(1, n2 + a1 * (in_plane(n2, kx1, ky1, v1) - (k01 + k12) * n2 + k01 * e2))
    g, e = ghost_c[2] + d2, own_c[2] + e2
    flow = k_face * (g - e)
    finish(
        0,
        e2
        + a0
        * (
            in_plane(e2, kx0, ky0, v0) - hold * e2 + k01 * n2
            + (flow + couple(m_ref, to_own, g))
        ),
    )
    for copy in copies:
        copy.wait()


def swap(value, axis, parity):
    count = lax.axis_size(axis)
    pairs = []
    for i in range(parity, count - 1, 2):
        pairs += [(i, i + 1), (i + 1, i)]
    return lax.ppermute(value, axis, pairs)


def shape(*dims):
    return jax.ShapeDtypeStruct(dims, jnp.float32)


def call(kernel, outs, scratch=(), **specs):
    return pl.pallas_call(
        kernel,
        out_shape=outs,
        scratch_shapes=list(scratch),
        cost_estimate=pl.CostEstimate(flops=1024, bytes_accessed=1024, transcendentals=0),
        compiler_params=pltpu.CompilerParams(vmem_limit_bytes=40 * 2**20),
        **specs,
    )


def per_device(conc, kappa, velocity, cell_type, target_row, target_col, mortar_weight):
    tile = (ROWS, COLS)
    plane = (COLS, LANES)
    tall = (TALL, LANES)
    given = (conc, kappa, velocity, cell_type, target_row, target_col, mortar_weight)
    anywhere = pl.BlockSpec(memory_space=pl.ANY)
    whole = pl.BlockSpec(memory_space=pltpu.VMEM)

    msg_a, msg_b, raw_a, raw_b, *fields, faces = call(
        pack_kernel,
        [shape(GROUPS, EDGE, LANES)] * 2
        + [shape(RAW, *plane)] * 2
        + [shape(DEPTH, *plane)] * 3
        + [shape(6, *plane)],
        [pltpu.VMEM(x.shape, x.dtype) for x in given] + [pltpu.SemaphoreType.DMA((7,))],
        in_specs=[anywhere] * 7,
    )(*[pltpu.with_memory_space_constraint(x, pltpu.HBM) for x in given])
    got_b = swap(msg_b, "stream", 1)
    got_a = swap(msg_a, "stream", 0)
    raw_b = swap(raw_b, "slab", 1)
    raw_a = swap(raw_a, "slab", 0)
    fields += [got_a, got_b]
    late_b, edge_b, m = call(
        functools.partial(edge_kernel, 1),
        (shape(LATE + EDGE, LANES), shape(2, *tall), shape(11, *tall)),
    )(*fields, faces)
    late_b = swap(late_b, "slab", 1)
    late_a, edge_a = call(
        functools.partial(edge_kernel, 0), (shape(LATE, LANES), shape(2, *tall))
    )(*fields, m)
    late_a = swap(late_a, "slab", 0)
    u3, middle, coef, av, both_m = call(
        block_kernel,
        (
            shape(DEPTH, *plane),
            shape(2, DEPTH - 6, *tile),
            shape(2, 10, *tall),
            shape(2, 5, *tall),
            shape(2, 10, *tall),
        ),
        (
            pltpu.VMEM((2, DEPTH) + tall, jnp.float32),
            pltpu.VMEM((DEPTH,) + tall, jnp.float32),
            pltpu.VMEM((DEPTH,) + tall, jnp.float32),
            pltpu.VMEM((DEPTH,) + tall, jnp.float32),
            pltpu.VMEM((2,) + tall, jnp.float32),
            pltpu.VMEM((DEPTH,) + tall, jnp.float32),
            pltpu.VMEM((DEPTH,) + tall, jnp.float32),
        ),
    )(*fields, m)

    def join(parity, operands, extra, outs, **specs):
        return call(
            functools.partial(join_kernel, parity),
            outs,
            in_specs=[whole] * (4 + len(operands)) + [anywhere] * len(extra),
            **specs,
        )(coef, av, operands[0], both_m, u3, *operands[1:], *extra)

    joined = join(0, (edge_a, raw_a, late_a), (raw_b,), shape(2, 3, *tile))
    return join(
        1,
        (edge_b, raw_b, late_b, joined, middle),
        (),
        shape(2, DEPTH, *tile),
        scratch=(pltpu.VMEM((2, 3) + tile, jnp.float32), pltpu.SemaphoreType.DMA((7,))),
        out_specs=anywhere,
    )


def solution(mesh):
    return jax.shard_map(
        per_device,
        mesh=mesh,
        in_specs=(
            P(None, "slab", None, "stream"),
            P(None, "slab", None, "stream"),
            P("slab", None, "stream"),
            P("slab", None, "stream"),
            P(None, None, "stream"),
            P(None, None, "stream"),
            P(None, None, "stream"),
        ),
        out_specs=P(None, "slab", None, "stream"),
        check_vma=False,
    )
```
